512 devices in a mesh: seq: 64 (over z, y), heads: 8 (over x, core).
Axes of the slice: x: 4, y: 8, z: 8, core: 2. Of those that a mesh axis runs over, the one named last changes fastest.
Arguments:
- self_queries: bfloat16 [8192, 2048], P('seq', 'heads'), may hold values from -200 to 200
- self_keys: bfloat16 [8192, 2048], P('seq', 'heads'), may hold values from -8 to 8
- self_values: bfloat16 [8192, 2048], P('seq', 'heads'), may hold values from -6 to 6
- cross_queries: bfloat16 [8192, 2048], P('seq', 'heads'), may hold values from -200 to 200
- store_keys: bfloat16 [256, 128, 2048], P(None, 'seq', 'heads'), may hold values from -8 to 8
- store_values: bfloat16 [256, 128, 2048], P(None, 'seq', 'heads'), may hold values from -6 to 6
- neighbour_ids: int32 [128, 2], replicated, may hold values from 0 to 255
- out_weight: bfloat16 [2048, 4096], P('heads'), may hold values from -0.125 to 0.125
- grad_out: bfloat16 [8192, 4096], P('seq'), may hold values from -6 to 6
Outputs:
- self_out: bfloat16 [8192, 2048], P('seq', 'heads')
- projected: bfloat16 [8192, 4096], P('seq', 'heads')
- grad_cross_queries: float32 [8192, 2048], P('seq', 'heads')
- grad_store_keys: bfloat16 [256, 128, 2048], P(None, 'seq', 'heads')
- grad_store_values: bfloat16 [256, 128, 2048], P(None, 'seq', 'heads')
The draws below stay inside these ranges and needn't reach their ends.
All inputs are finite; a program needn't handle non-finite values.
Results may differ from the reference program's by a relative error of at most 0.019.
Values may be sent and summed in bfloat16 or wider, within the bound.
A program may use at most 64 MiB of HBM per device.

```python
import math
import jax
import jax.numpy as jnp
import numpy as np
from jax import lax

D = 4096
HEAD_DIM = 128
SPAN = 64
NEIGH = 2
NROWS = 128
HEADS = 16
TOKENS = 8192
SPANS = 128
NBLK = 256


def drawn_normal(key, shape):
    return jnp.clip(jax.random.normal(key, shape, jnp.float32), -6.0, 6.0)


def draw_self_keys(key, part):
    key = jax.random.fold_in(key, 1)
    drawn = drawn_normal(key, (TOKENS, HEADS * HEAD_DIM))
    return drawn.astype(jnp.bfloat16)


def draw_self_queries(key, part):
    key = jax.random.fold_in(key, 2)
    drawn = drawn_normal(key, (TOKENS, HEADS * HEAD_DIM))
    return drawn.astype(jnp.bfloat16)


def draw_store_keys(key, part):
    key = jax.random.fold_in(key, 3)
    drawn = drawn_normal(key, (NBLK, NROWS, HEADS * HEAD_DIM))
    return drawn.astype(jnp.bfloat16)


def draw_cross_queries(key, part):
    key = jax.random.fold_in(key, 4)
    drawn = drawn_normal(key, (TOKENS, HEADS * HEAD_DIM))
    return drawn.astype(jnp.bfloat16)


def with_ends(values, own_key, smallest, largest):
    extent = values.shape
    spot = [jax.random.randint(jax.random.fold_in(own_key, axis), (), 0, extent[axis]) for axis in range(len(extent))]
    values = values.at[tuple(spot)].set(smallest)
    longest = extent.index(max(extent))
    spot[longest] = (spot[longest] + 1) % extent[longest]
    return values.at[tuple(spot)].set(largest)


def block_scale(own_key, dims, cuts, least, top_value):
    def one(position, blocks):
        steps = jax.random.uniform(jax.random.fold_in(jax.random.fold_in(own_key, 6), position), (blocks,), jnp.float32, least / len(cuts), top_value / len(cuts))
        return jnp.repeat(jnp.exp(steps), dims[position] // blocks).reshape((-1,) + (1,) * (len(dims) - position - 1))

    factor_of = one(*cuts[0])
    for cut in cuts[1:]:
        factor_of = factor_of * one(*cut)
    return factor_of


def cumulative_ranks(amount, lean):
    portions = [(1 << 20) // math.isqrt(rank ** lean) + 1 for rank in range(1, amount + 1)]
    deviation = 1 + sum(portions) // (1 << 30)
    return np.cumsum(np.array([max(1, weight // deviation) for weight in portions]))


def ranked(rng, extent, count, slope):
    table = cumulative_ranks(count, slope)
    pick = jax.random.randint(jax.random.fold_in(rng, 1), extent, 0, int(table[count - 1]))
    rank = jnp.searchsorted(jnp.asarray(table, jnp.int32), pick, side="right")
    return jax.random.permutation(jax.random.fold_in(rng, 2), count)[rank].astype(jnp.int32)


def centred(rng, extent, width, most, cuts=(), kind=jnp.bfloat16):
    values = width * jax.random.normal(rng, extent, jnp.float32)
    if cuts:
        values = values * block_scale(rng, extent, cuts, -0.22, 0.18)
    return jnp.clip(values, -most, most).astype(kind)


def setup_inputs(seed: int = 0) -> dict:
    streams_of = jax.random.split(jax.random.key(seed), 10)
    self_queries = draw_self_queries(jax.random.fold_in(streams_of[9], 71), 0)
    self_keys = draw_self_keys(jax.random.fold_in(streams_of[9], 71), 0)
    self_values = centred(streams_of[2], (TOKENS, HEADS * HEAD_DIM), 1.0, 6.0, ((0, 64), (1, 8)))
    cross_queries = draw_cross_queries(jax.random.fold_in(streams_of[9], 71), 0)
    store_keys = draw_store_keys(jax.random.fold_in(streams_of[9], 71), 0)
    store_values = centred(streams_of[5], (NBLK, NROWS, HEADS * HEAD_DIM), 1.0, 6.0, ((1, 64), (2, 8)))
    neighbour_ids = with_ends(ranked(streams_of[6], (SPANS, NEIGH), NBLK, 2), jax.random.fold_in(streams_of[6], 3), 0, NBLK - 1).astype(jnp.int32)
    out_weight = centred(streams_of[7], (HEADS * HEAD_DIM, D), (HEADS * HEAD_DIM) ** -0.5, 0.125, ((0, 8),))
    grad_out = centred(streams_of[8], (TOKENS, D), 1.0, 6.0, ((0, 64),))
    return dict(self_queries=self_queries, self_keys=self_keys, self_values=self_values, cross_queries=cross_queries, store_keys=store_keys, store_values=store_values, neighbour_ids=neighbour_ids, out_weight=out_weight, grad_out=grad_out)


def self_head(head_queries, head_keys, head_values):
    score_scale = 1.0 / math.sqrt(HEAD_DIM)
    block_rows = math.gcd(TOKENS, 512)
    key_position = jnp.arange(TOKENS, dtype=jnp.int32)

    def one_block(block_index):
        first_row = block_index * block_rows
        query_rows = lax.dynamic_slice_in_dim(head_queries, first_row, block_rows, 0)
        scores = jnp.dot(query_rows, head_keys.T, preferred_element_type=jnp.float32) * score_scale
        query_position = first_row + jnp.arange(block_rows, dtype=jnp.int32)
        allowed = key_position[None, :] <= query_position[:, None]
        masked = jnp.where(allowed, scores, -jnp.inf)
        row_max = lax.optimization_barrier(jnp.max(masked, axis=1, keepdims=True))
        numerators = jnp.where(allowed, jnp.exp(masked - row_max), 0.0)
        row_sum = lax.optimization_barrier(jnp.sum(numerators, axis=1, keepdims=True))
        blended = jnp.dot(numerators.astype(jnp.bfloat16), head_values, preferred_element_type=jnp.float32)
        return (blended / row_sum).astype(jnp.bfloat16)
    head_out = lax.map(one_block, jnp.arange(TOKENS // block_rows, dtype=jnp.int32))
    return head_out.reshape(TOKENS, HEAD_DIM)

def split_heads(rows):
    return rows.reshape(TOKENS, HEADS, HEAD_DIM).transpose(1, 0, 2)

def cross_group(query_rows, grad_rows, group_ids, matched, store_keys, store_values):
    score_scale = 1.0 / math.sqrt(HEAD_DIM)
    near_keys = store_keys[group_ids].reshape(NEIGH * NROWS, HEADS, HEAD_DIM)
    near_values = store_values[group_ids].reshape(NEIGH * NROWS, HEADS, HEAD_DIM)
    query_float = query_rows.astype(jnp.float32)
    grad_float = grad_rows.astype(jnp.float32)
    key_float = near_keys.astype(jnp.float32)
    value_float = near_values.astype(jnp.float32)
    scores = jnp.einsum('qhd,khd->hqk', query_float, key_float) * score_scale
    row_max = lax.optimization_barrier(jnp.max(scores, axis=2, keepdims=True))
    numerators = jnp.exp(scores - row_max)
    cross_probs = numerators / lax.optimization_barrier(jnp.sum(numerators, axis=2, keepdims=True))
    cross_weights = lax.optimization_barrier(cross_probs.astype(jnp.bfloat16)).astype(jnp.float32)
    cross_out = (jnp.einsum('hqk,khd->qhd', cross_weights, value_float) * matched).astype(jnp.bfloat16)
    grad_probs = jnp.einsum('qhd,khd->hqk', grad_float, value_float)
    grad_scores = cross_probs * (grad_probs - lax.optimization_barrier(jnp.sum(cross_probs * grad_probs, axis=2, keepdims=True)))
    grad_weights = lax.optimization_barrier(grad_scores.astype(jnp.bfloat16)).astype(jnp.float32)
    query_grads = jnp.einsum('hqk,khd->qhd', grad_weights, key_float) * score_scale
    key_grads = jnp.einsum('hqk,qhd->khd', grad_weights, query_float) * score_scale
    value_grads = jnp.einsum('hqk,qhd->khd', cross_weights, grad_float)
    return (cross_out, query_grads, key_grads, value_grads)

def reference(self_queries, self_keys, self_values, cross_queries, store_keys, store_values, neighbour_ids, out_weight, grad_out):
    full_width = HEADS * HEAD_DIM
    heads_out = lax.map(lambda parts: self_head(parts[0], parts[1], parts[2]), (split_heads(self_queries), split_heads(self_keys), split_heads(self_values)))
    self_out = heads_out.transpose(1, 0, 2).reshape(TOKENS, full_width)
    group_count = SPANS + 1
    token_matched = ((jnp.arange(TOKENS, dtype=jnp.int32) + 1) // SPAN >= 1).astype(jnp.float32)
    grad_cross = jnp.dot(grad_out, out_weight.T, preferred_element_type=jnp.float32)
    grad_cross = (grad_cross * token_matched[:, None]).astype(jnp.bfloat16)

    def grouped(rows):
        pad_front = jnp.zeros((1, full_width), rows.dtype)
        pad_back = jnp.zeros((SPAN - 1, full_width), rows.dtype)
        joined = jnp.concatenate([pad_front, rows, pad_back], axis=0)
        return joined.reshape(group_count, SPAN, HEADS, HEAD_DIM)
    padded_ids = jnp.concatenate([jnp.zeros((1, NEIGH), jnp.int32), neighbour_ids.astype(jnp.int32)], axis=0)
    group_matched = (jnp.arange(group_count, dtype=jnp.int32) >= 1).astype(jnp.float32)

    def one_group(parts):
        return cross_group(parts[0], parts[1], parts[2], parts[3], store_keys, store_values)
    cross_out, query_grads, key_grads, value_grads = lax.map(one_group, (grouped(cross_queries), grouped(grad_cross), padded_ids, group_matched))
    cross_rows = cross_out.reshape(group_count * SPAN, full_width)[1:TOKENS + 1]
    projected = jnp.dot(cross_rows, out_weight, preferred_element_type=jnp.float32).astype(jnp.bfloat16)
    grad_cross_queries = query_grads.reshape(group_count * SPAN, full_width)[1:TOKENS + 1]
    flat_ids = padded_ids.reshape(group_count * NEIGH)
    key_terms = key_grads.reshape(group_count * NEIGH, NROWS * full_width)
    value_terms = value_grads.reshape(group_count * NEIGH, NROWS * full_width)
    grad_store_keys = jax.ops.segment_sum(key_terms, flat_ids, num_segments=NBLK)
    grad_store_values = jax.ops.segment_sum(value_terms, flat_ids, num_segments=NBLK)
    grad_store_keys = grad_store_keys.reshape(NBLK, NROWS, full_width).astype(jnp.bfloat16)
    grad_store_values = grad_store_values.reshape(NBLK, NROWS, full_width).astype(jnp.bfloat16)
    return (self_out, projected, grad_cross_queries, grad_store_keys, grad_store_values)
```

```python
import functools
import math

import jax
import jax.numpy as jnp
from jax import lax
from jax.experimental import pallas as pl
from jax.experimental.pallas import tpu as pltpu
from jax.sharding import PartitionSpec as P

MESH = pl.DeviceIdType.MESH
BF16 = jnp.bfloat16
F32 = jnp.float32
HEAD_DIM = 128
SCALE = 1.0 / math.sqrt(HEAD_DIM)
LOW = -1e30
Z_CHUNKS = 4
Y_CHUNKS = 2


def dot(a, b, dims):
    return lax.dot_general(a, b, (dims, ((), ())), preferred_element_type=F32)


def iota(shape, axis):
    return lax.broadcasted_iota(jnp.int32, shape, axis)


def remote(src, dst, send_sem, recv_sem, device):
    return pltpu.make_async_remote_copy(
        src_ref=src,
        dst_ref=dst,
        send_sem=send_sem,
        recv_sem=recv_sem,
        device_id=device,
        device_id_type=MESH,
    )


def shifted_seq(s, dz, dy):
    return lax.rem(s // 8 + dz, 8) * 8 + lax.rem(lax.rem(s, 8) + dy, 8)


class Ring:
    def __init__(self, buf, send_sem, recv_sem, right, left, chunks):
        self.buf, self.send_sem, self.recv_sem = buf, send_sem, recv_sem
        self.right, self.left, self.chunks = right, left, chunks
        self.rows = buf.shape[1] // chunks

    def copy(self, step, rightward, chunk):
        source, target = (step - 1, step) if rightward else ((9 - step) % 8, 8 - step)
        rows = pl.ds(chunk * self.rows, self.rows)
        return remote(
            self.buf.at[source, rows],
            self.buf.at[target, rows],
            self.send_sem.at[int(rightward), step, chunk],
            self.recv_sem.at[int(rightward), step, chunk],
            self.right if rightward else self.left,
        )

    def moves(self, step):
        half = self.chunks // 2
        return [
            (rightward, chunk)
            for chunk in range(self.chunks)
            for rightward in (True, False)
            if step < 4 or (chunk < half) == rightward
        ]

    def run_step(self, step):
        for rightward, chunk in self.moves(step):
            if step > 1:
                self.copy(step - 1, rightward, chunk).wait_recv()
            self.copy(step, rightward, chunk).start()

    def finish(self):
        for rightward, chunk in self.moves(4):
            self.copy(4, rightward, chunk).wait_recv()
        for rightward, chunk in self.moves(3):
            if (rightward, chunk) not in self.moves(4):
                self.copy(3, rightward, chunk).wait_recv()
        for step in range(1, 5):
            for rightward, chunk in self.moves(step):
                self.copy(step, rightward, chunk).wait_send()


def body(
    sq_in, sk_in, sv_in, cq_in, stk_in, stv_in, idt, w_in, go_in,
    self_out, projected, grad_q, grad_k, grad_v,
    kv, qb, cq, stk, stv, w, go,
    sel_t, sb, rb, gs, gr, gc, shift_s, shift_r, back_s, back_r,
    acc, top, total, o_s, o_r, stat_s, stat_r, part_s, part_r,
    load_sem, z_ss, z_rs, y_ss, y_rs, sems,
):
    s, h = lax.axis_index("seq"), lax.axis_index("heads")
    z, y = s // 8, lax.rem(s, 8)

    def load(i, src, dst):
        return pltpu.make_async_copy(src, dst, load_sem.at[i])

    loads = [
        load(0, stk_in, stk),
        load(1, stv_in, stv),
        load(2, go_in, go),
        load(3, w_in, w),
        load(4, sk_in, kv.at[0, pl.ds(0, 128)]),
        load(5, sv_in, kv.at[0, pl.ds(128, 128)]),
        load(6, sq_in, qb.at[0]),
        load(7, cq_in, cq),
    ]
    for copy in loads:
        copy.start()

    barrier = pltpu.get_barrier_semaphore()

    def greet_seq(k, _):
        device = (shifted_seq(s, k // 8, lax.rem(k, 8)), h)
        pl.semaphore_signal(barrier, inc=1, device_id=device, device_id_type=MESH)
        return 0

    def greet_heads(k, _):
        device = (s, lax.rem(h + k, 8))
        pl.semaphore_signal(barrier, inc=1, device_id=device, device_id_type=MESH)
        return 0

    lax.fori_loop(1, 64, greet_seq, 0)
    lax.fori_loop(1, 8, greet_heads, 0)

    ids = idt[...].astype(F32)
    first_id = jnp.broadcast_to(ids[0:1], (128, 128)).astype(BF16)
    second_id = jnp.broadcast_to(ids[1:2], (128, 128)).astype(BF16)
    sub, lane = iota((512, 128), 0), iota((512, 128), 1)
    span_of = (lane == (((sub >> 2) + 127) & 127)).astype(F32).astype(BF16)
    picked = jnp.where(
        (sub & 2) == 0,
        dot(span_of, first_id, ((1,), (1,))),
        dot(span_of, second_id, ((1,), (1,))),
    )
    wanted = picked * 2.0 + (sub & 1).astype(F32)
    lane_f = lane.astype(F32)
    sel = jnp.concatenate(
        [jnp.where(wanted == lane_f + 128.0 * c, 1.0, 0.0).astype(BF16) for c in range(4)], axis=1
    )
    loads[0].wait()
    keys_out = dot(sel, stk[...].reshape(512, 256), ((1,), (0,)))
    loads[1].wait()
    values_out = dot(sel, stv[...].reshape(512, 256), ((1,), (0,)))
    sb[...] = jnp.concatenate(
        [keys_out.reshape(64, 8, 256), values_out.reshape(64, 8, 256)], axis=1
    ).astype(BF16)
    rb[pl.ds(s, 1)] = sb[pl.ds(s, 1)]

    loads[2].wait()
    loads[3].wait()
    gc[...] = dot(go[...], w[...], ((1,), (1,))).astype(BF16)
    loads[7].wait()
    shift_s[pl.ds(0, 16)] = cq[pl.ds(112, 16)]
    shift_s[pl.ds(16, 16)] = gc[pl.ds(112, 16)]
    loads[4].wait()
    loads[5].wait()
    loads[6].wait()

    pl.semaphore_wait(barrier, 70)

    def start_all(source, target, which):
        def one(k, _):
            to = shifted_seq(s, k // 8, lax.rem(k, 8))
            remote(source.at[to], target.at[s], sems.at[which], sems.at[which + 1], (to, h)).start()
            return 0

        lax.fori_loop(1, 64, one, 0)

    def wait_all(source, target, which):
        rows = pl.ds(0, 63)
        remote(
            source.at[rows],
            target.at[rows],
            sems.at[which],
            sems.at[which + 1],
            (shifted_seq(s, 0, 1), h),
        ).wait()

    after = (lax.rem(s + 1, 64), h)
    before = (lax.rem(s + 63, 64), h)
    ahead = remote(shift_s, shift_r, sems.at[0], sems.at[1], after)
    ahead.start()
    start_all(sb, rb, 2)
    z_ring = Ring(
        kv, z_ss, z_rs, (shifted_seq(s, 1, 0), h), (shifted_seq(s, 7, 0), h), Z_CHUNKS
    )
    y_ring = Ring(
        qb, y_ss, y_rs, (shifted_seq(s, 0, 1), h), (shifted_seq(s, 0, 7), h), Y_CHUNKS
    )
    for step in range(1, 5):
        z_ring.run_step(step)
        y_ring.run_step(step)

    sub_w, lane_w = iota((128, 512), 0), iota((128, 512), 1)
    span_row = (sub_w == (((lane_w >> 2) + 127) & 127)).astype(F32).astype(BF16)
    lane_8 = iota((8, 512), 1)
    picked_row = jnp.where(
        (lane_8 & 2) == 0,
        dot(first_id[0:8], span_row, ((1,), (0,))),
        dot(second_id[0:8], span_row, ((1,), (0,))),
    )
    wanted_row = (picked_row * 2.0 + (lane_8 & 1).astype(F32))[0:1]
    sel_t[...] = jnp.where(iota((512, 512), 0).astype(F32) == wanted_row, 1.0, 0.0).astype(BF16)

    ahead.wait()
    row_1 = iota((128, 256), 0)
    shifted_in = shift_r[...].astype(F32)
    queries = jnp.where(
        row_1 == 0, shifted_in[15:16], pltpu.roll(cq[...].astype(F32), 1, 0)
    ).astype(BF16)
    place = row_1 + s * 128
    unmatched = (place >= 1) & (place < 64)
    grads = jnp.where(row_1 == 0, shifted_in[31:32], pltpu.roll(gc[...].astype(F32), 1, 0))
    grads = jnp.where(unmatched, 0.0, grads).astype(BF16)
    wait_all(sb, rb, 2)
    got = rb[...].astype(F32)
    near_keys = got[:, :8].reshape(512, 256).astype(BF16)
    near_values = got[:, 8:].reshape(512, 256).astype(BF16)
    mine = ((iota((512, 128), 0) & 4) != 0) == (iota((512, 128), 1) >= 64)
    outs, query_grads, key_grads, value_grads = [], [], [], []
    for head in range(2):
        cols = slice(head * 128, head * 128 + 128)
        k_h, v_h, q_h, g_h = near_keys[:, cols], near_values[:, cols], queries[:, cols], grads[:, cols]
        scores = jnp.where(mine, dot(k_h, q_h, ((1,), (1,))) * SCALE, LOW)
        numer = jnp.exp(scores - jnp.max(scores, axis=0, keepdims=True))
        probs = numer / jnp.sum(numer, axis=0, keepdims=True)
        weights = probs.astype(BF16)
        outs.append(dot(weights, v_h, ((0,), (0,))))
        grad_probs = dot(v_h, g_h, ((1,), (1,)))
        centre = jnp.sum(probs * grad_probs, axis=0, keepdims=True)
        grad_weights = (probs * (grad_probs - centre)).astype(BF16)
        query_grads.append(dot(grad_weights, k_h, ((0,), (0,))) * SCALE)
        key_grads.append(dot(grad_weights, q_h, ((1,), (0,))) * SCALE)
        value_grads.append(dot(weights, g_h, ((1,), (0,))))
    key_grads = jnp.concatenate(key_grads, axis=1).reshape(64, 8, 256)
    value_grads = jnp.concatenate(value_grads, axis=1).reshape(64, 8, 256)
    gs[...] = jnp.concatenate([key_grads, value_grads], axis=1).astype(BF16)
    gr[pl.ds(s, 1)] = gs[pl.ds(s, 1)]
    start_all(gs, gr, 4)
    cross = jnp.where(unmatched, 0.0, jnp.concatenate(outs, axis=1))
    query_grads = jnp.concatenate(query_grads, axis=1)
    back_s[...] = jnp.concatenate([cross[0:8], query_grads[0:8]], axis=1)
    back = remote(back_s, back_r, sems.at[6], sems.at[7], before)
    back.start()

    z_ring.finish()
    y_ring.finish()

    def attend(d, first):
        for head in range(2):
            cols = pl.ds(head * 128, 128)
            k_h = kv[pl.ds(d, 1), pl.ds(0, 128), cols].reshape(128, 128)
            v_h = kv[pl.ds(d, 1), pl.ds(128, 128), cols].reshape(128, 128)
            q_h = qb[:, :, cols].reshape(1024, 128)
            scores = dot(k_h, q_h, ((1,), (1,))) * SCALE
            if first:
                key, query = iota((128, 1024), 0), iota((128, 1024), 1)
                block = query >> 7
                allowed = ((block == 0) & (key <= query)) | (block > y)
                scores = jnp.where(allowed, scores, LOW)
                top_new = jnp.max(scores, axis=0, keepdims=True)
                numer = jnp.where(allowed, jnp.exp(scores - top_new), 0.0)
                total[head] = jnp.sum(numer, axis=0, keepdims=True)
                acc[head] = dot(v_h, numer.astype(BF16), ((0,), (0,)))
            else:
                top_old = top[head]
                top_new = jnp.maximum(top_old, jnp.max(scores, axis=0, keepdims=True))
                fade = jnp.exp(top_old - top_new)
                numer = jnp.exp(scores - top_new)
                total[head] = total[head] * fade + jnp.sum(numer, axis=0, keepdims=True)
                acc[head] = acc[head] * fade + dot(v_h, numer.astype(BF16), ((0,), (0,)))
            top[head] = top_new

    attend(0, True)

    def later_block(d, _):
        attend(d, False)
        return 0

    lax.fori_loop(1, z + 1, later_block, 0)
    for e in range(8):
        cols = slice(e * 128, e * 128 + 128)
        o_s[e] = jnp.concatenate([acc[0, :, cols], acc[1, :, cols]], axis=0).astype(BF16)
        stat_s[e] = jnp.concatenate(
            [top[0, :, cols], total[0, :, cols], top[1, :, cols], total[1, :, cols], jnp.zeros((4, 128), F32)],
            axis=0,
        )
    for e in (4, 3, 5, 2, 6, 1, 7):
        owner = (shifted_seq(s, 0, 8 - e), h)
        remote(o_s.at[e], o_r.at[e], sems.at[8], sems.at[9], owner).start()
        remote(stat_s.at[e], stat_r.at[e], sems.at[10], sems.at[11], owner).start()

    back.wait()
    came_back = back_r[...]
    last = row_1 == 127
    grad_q[...] = jnp.where(last, came_back[0:1, 256:], pltpu.roll(query_grads, 127, 0))
    cross_rows = jnp.where(last, came_back[0:1, :256], pltpu.roll(cross, 127, 0)).astype(BF16)

    def project(c, _):
        cols = pl.ds(pl.multiple_of(c * 512, 512), 512)
        part_s[pl.ds(c, 1)] = dot(cross_rows, w[:, cols], ((1,), (0,))).astype(BF16)[None]
        return 0

    lax.fori_loop(0, 8, project, 0)
    for k in (4, 3, 5, 2, 6, 1, 7):
        owner = lax.rem(h + k, 8)
        remote(part_s.at[owner], part_r.at[k], sems.at[12], sems.at[13], (s, owner)).start()

    others = pl.ds(1, 7)
    neighbour = (shifted_seq(s, 0, 1), h)
    remote(o_s.at[others], o_r.at[others], sems.at[8], sems.at[9], neighbour).wait()
    remote(stat_s.at[others], stat_r.at[others], sems.at[10], sems.at[11], neighbour).wait()
    merged = []
    for head in range(2):
        tops = [(stat_s if e == 0 else stat_r)[e, 2 * head : 2 * head + 1] for e in range(8)]
        totals = [(stat_s if e == 0 else stat_r)[e, 2 * head + 1 : 2 * head + 2] for e in range(8)]
        best = functools.reduce(jnp.maximum, tops)
        fades = [jnp.exp(t - best) for t in tops]
        whole = sum(t * f for t, f in zip(totals, fades))
        summed = sum(
            (o_s if e == 0 else o_r)[e, head * 128 : head * 128 + 128].astype(F32) * fades[e]
            for e in range(8)
        )
        merged.append(jnp.transpose(summed / whole))
    self_out[...] = jnp.concatenate(merged, axis=1).astype(BF16)

    remote(
        part_s.at[others], part_r.at[others], sems.at[12], sems.at[13], (s, lax.rem(h + 1, 8))
    ).wait()
    summed = part_s[pl.ds(h, 1)].reshape(128, 512).astype(F32)
    for k in range(1, 8):
        summed += part_r[k].astype(F32)
    projected[...] = summed.astype(BF16)

    wait_all(gs, gr, 4)
    returned = gr[...].astype(F32)
    chosen = sel_t[...]
    for out, piece in ((grad_k, returned[:, :8]), (grad_v, returned[:, 8:])):
        rows = piece.reshape(512, 256).astype(BF16)
        out[...] = dot(chosen, rows, ((1,), (0,))).astype(BF16).reshape(256, 2, 256)


def shards(sq, sk, sv, cq, store_k, store_v, ids, w, go):
    any_space = pl.BlockSpec(memory_space=pl.ANY)
    vmem = pl.BlockSpec(memory_space=pltpu.VMEM)
    V = pltpu.VMEM
    dma = pltpu.SemaphoreType.DMA
    return pl.pallas_call(
        body,
        name="retrieval_attention",
        out_shape=(
            jax.ShapeDtypeStruct((128, 256), BF16),
            jax.ShapeDtypeStruct((128, 512), BF16),
            jax.ShapeDtypeStruct((128, 256), F32),
            jax.ShapeDtypeStruct((256, 2, 256), BF16),
            jax.ShapeDtypeStruct((256, 2, 256), BF16),
        ),
        in_specs=[any_space] * 6 + [vmem] + [any_space] * 2,
        out_specs=(vmem,) * 5,
        scratch_shapes=[
            V((8, 256, 256), BF16),
            V((8, 128, 256), BF16),
            V((128, 256), BF16),
            V((256, 2, 256), BF16),
            V((256, 2, 256), BF16),
            V((256, 4096), BF16),
            V((128, 4096), BF16),
            V((512, 512), BF16),
            V((64, 16, 256), BF16),
            V((64, 16, 256), BF16),
            V((64, 16, 256), BF16),
            V((64, 16, 256), BF16),
            V((128, 256), BF16),
            V((32, 256), BF16),
            V((32, 256), BF16),
            V((8, 512), F32),
            V((8, 512), F32),
            V((2, 128, 1024), F32),
            V((2, 1, 1024), F32),
            V((2, 1, 1024), F32),
            V((8, 256, 128), BF16),
            V((8, 256, 128), BF16),
            V((8, 8, 128), F32),
            V((8, 8, 128), F32),
            V((8, 128, 512), BF16),
            V((8, 128, 512), BF16),
            dma((8,)),
            dma((2, 5, Z_CHUNKS)),
            dma((2, 5, Z_CHUNKS)),
            dma((2, 5, Y_CHUNKS)),
            dma((2, 5, Y_CHUNKS)),
            dma((14,)),
        ],
        compiler_params=pltpu.CompilerParams(
            collective_id=0, has_side_effects=True, vmem_limit_bytes=50 << 20
        ),
    )(sq, sk, sv, cq, store_k, store_v, ids.T, w, go)


def solution(mesh):
    by_token = P("seq", "heads")
    by_row = P(None, "seq", "heads")
    return jax.shard_map(
        shards,
        mesh=mesh,
        in_specs=(
            by_token, by_token, by_token, by_token, by_row, by_row, P(), P("heads", None), P("seq", None),
        ),
        out_specs=(by_token, by_token, by_token, by_row, by_row),
        check_vma=False,
    )
```

```python
import functools
import math

import jax
import jax.numpy as jnp
from jax import lax
from jax.experimental import pallas as pl
from jax.experimental.pallas import tpu as pltpu
from jax.sharding import PartitionSpec as P

MESH = pl.DeviceIdType.MESH
BF16 = jnp.bfloat16
F32 = jnp.float32
HEAD_DIM = 128
SCALE = 1.0 / math.sqrt(HEAD_DIM)
LOW = -1e30
CHUNKS = 2


def dot(a, b, dims):
    return lax.dot_general(a, b, (dims, ((), ())), preferred_element_type=F32)


def iota(shape, axis):
    return lax.broadcasted_iota(jnp.int32, shape, axis)


def remote(src, dst, send_sem, recv_sem, device):
    return pltpu.make_async_remote_copy(
        src_ref=src,
        dst_ref=dst,
        send_sem=send_sem,
        recv_sem=recv_sem,
        device_id=device,
        device_id_type=MESH,
    )


def shifted_seq(s, dz, dy):
    return lax.rem(s // 8 + dz, 8) * 8 + lax.rem(lax.rem(s, 8) + dy, 8)


def far_first(i):
    return lax.rem(4 + (1 - 2 * lax.rem(i, 2)) * ((i + 1) // 2), 8)


class Ring:
    def __init__(self, own, buf, send_sem, recv_sem, right, left):
        self.own = own
        self.buf, self.send_sem, self.recv_sem = buf, send_sem, recv_sem
        self.right, self.left = right, left
        self.rows = buf.shape[1] // CHUNKS

    def copy(self, step, rightward, chunk):
        source, target = (step - 1, step) if rightward else ((9 - step) % 8, 8 - step)
        rows = pl.ds(chunk * self.rows, self.rows)
        return remote(
            self.buf.at[source, rows],
            self.buf.at[target, rows],
            self.send_sem.at[int(rightward), step, chunk],
            self.recv_sem.at[int(rightward), step, chunk],
            self.right if rightward else self.left,
        )

    def moves(self, step):
        return [
            (rightward, chunk)
            for chunk in range(CHUNKS)
            for rightward in (True, False)
            if step < 4 or (chunk < CHUNKS // 2) == rightward
        ]

    def finish(self):
        for rightward, chunk in self.moves(4):
            self.copy(4, rightward, chunk).wait_recv()
        for rightward, chunk in self.moves(3):
            if (rightward, chunk) not in self.moves(4):
                self.copy(3, rightward, chunk).wait_recv()

    def finish_sends(self):
        for step in range(1, 5):
            for rightward, chunk in self.moves(step):
                self.copy(step, rightward, chunk).wait_send()


def run_step(rings, step):
    for rightward, chunk in rings[0].moves(step):
        for ring in rings:
            if step > 1:
                ring.copy(step - 1, rightward, chunk).wait_recv()
            ring.copy(step, rightward, chunk).start()


def body(
    sq_in, sk_in, sv_in, cq_in, stk_in, stv_in, idt, w_in, go_in,
    self_out, projected, grad_q, grad_k, grad_v,
    zr, yr, cq, stk, stv, w, go,
    sel_t, sb, rb, gs, gr, gc, shift_s, shift_r, back_s, back_r,
    acc, top, total, oy_s, oy_r, sy_s, sy_r, oz_s, oz_r, sz_s, sz_r, part_s, part_r, pair_s, pair_r, edge_r,
    so_v, pr_v, dq_v, dk_v, dv_v,
    load_sem, z_ss, z_rs, y_ss, y_rs, oz_ss, oz_rs, sz_ss, sz_rs, pair_ss, pair_rs, sems, out_sem, plane_sem,
):
    s, h = lax.axis_index("seq"), lax.axis_index("heads")
    z, y = s // 8, lax.rem(s, 8)
    low, high = pl.ds(0, 128), pl.ds(128, 128)
    k_rows, v_rows, q_rows = pl.ds(0, 128), pl.ds(128, 128), pl.ds(256, 128)

    barrier = pltpu.get_barrier_semaphore()

    def greet_lines(k, _):
        step = far_first(k)
        for device in ((shifted_seq(s, step, 0), h), (shifted_seq(s, 0, step), h)):
            pl.semaphore_signal(barrier, inc=1, device_id=device, device_id_type=MESH)
        return 0

    lax.fori_loop(0, 7, greet_lines, 0)
    x, core = h // 2, lax.rem(h, 2)
    sibling = (s, h + 1 - 2 * core)

    def same_core(row, dx):
        return (row, lax.rem(x + dx, 4) * 2 + core)

    near = [sibling] + [same_core(s, dx) for dx in (1, 2, 3)]
    near += [same_core(row, dx) for row in (lax.rem(s + 1, 64), lax.rem(s + 63, 64)) for dx in range(4)]
    for device in near:
        pl.semaphore_signal(barrier, inc=1, device_id=device, device_id_type=MESH)

    def load(i, src, dst):
        return pltpu.make_async_copy(src, dst, load_sem.at[i])

    z_own = (sk_in.at[:, low], sv_in.at[:, low], sq_in.at[:, high])
    y_own = (sk_in.at[:, high], sv_in.at[:, high], sq_in.at[:, low])
    parts = (k_rows, v_rows, q_rows)
    loads = [load(0, stk_in, stk), load(1, stv_in, stv), load(2, go_in, go), load(3, w_in, w), load(4, cq_in, cq)]
    loads += [load(5 + i, z_own[i], zr.at[0, parts[i]]) for i in range(3)]
    loads += [load(8 + i, y_own[i], yr.at[0, parts[i]]) for i in range(3)]
    for copy in loads[5:] + loads[:5]:
        copy.start()

    def halves(own):
        return [ref.at[pl.ds(half, 64)] for ref in own for half in (0, 64)]


    pl.semaphore_wait(barrier, 26)

    def greet_plane(k, _):
        device = (shifted_seq(s, far_first(k), 0), h)
        pl.semaphore_signal(plane_sem, inc=1, device_id=device, device_id_type=MESH)
        return 0

    lax.fori_loop(0, 7, greet_plane, 0)
    rings = (
        Ring(halves(z_own), zr, z_ss, z_rs, (shifted_seq(s, 1, 0), h), (shifted_seq(s, 7, 0), h)),
        Ring(halves(y_own), yr, y_ss, y_rs, (shifted_seq(s, 0, 1), h), (shifted_seq(s, 0, 7), h)),
    )
    for copy in loads[5:]:
        copy.wait()
    run_step(rings, 1)

    ids = idt[...].astype(F32)
    first_id = jnp.broadcast_to(ids[0:1], (128, 128)).astype(BF16)
    second_id = jnp.broadcast_to(ids[1:2], (128, 128)).astype(BF16)
    sub, lane = iota((512, 128), 0), iota((512, 128), 1)
    span_of = (lane == (((sub >> 2) + 127) & 127)).astype(F32).astype(BF16)
    picked = jnp.where(
        (sub & 2) == 0,
        dot(span_of, first_id, ((1,), (1,))),
        dot(span_of, second_id, ((1,), (1,))),
    )
    wanted = picked * 2.0 + (sub & 1).astype(F32)
    lane_f = lane.astype(F32)
    sel = jnp.concatenate(
        [jnp.where(wanted == lane_f + 128.0 * c, 1.0, 0.0).astype(BF16) for c in range(4)], axis=1
    )
    loads[0].wait()
    keys_out = dot(sel, stk[...].reshape(512, 256), ((1,), (0,)))
    loads[1].wait()
    values_out = dot(sel, stv[...].reshape(512, 256), ((1,), (0,)))
    sb[...] = jnp.concatenate(
        [keys_out.reshape(64, 8, 256), values_out.reshape(64, 8, 256)], axis=1
    ).astype(BF16)
    rb[pl.ds(s, 1)] = sb[pl.ds(s, 1)]


    def start_all(source, target, which):
        def one(k, _):
            to = shifted_seq(s, far_first(k // 8), far_first(lax.rem(k, 8)))
            remote(source.at[to], target.at[s], sems.at[which], sems.at[which + 1], (to, h)).start()
            return 0

        lax.fori_loop(0, 63, one, 0)

    def wait_all(source, target, which):
        rows = pl.ds(0, 63)
        remote(
            source.at[rows],
            target.at[rows],
            sems.at[which],
            sems.at[which + 1],
            (shifted_seq(s, 0, 1), h),
        ).wait()

    after = (lax.rem(s + 1, 64), h)
    before = (lax.rem(s + 63, 64), h)

    pl.semaphore_wait(plane_sem, 7)
    start_all(sb, rb, 2)

    run_step(rings, 2)


    run_step(rings, 3)

    loads[2].wait()
    loads[3].wait()
    gc[...] = dot(go[...], w[...], ((1,), (1,))).astype(BF16)
    loads[4].wait()
    shift_s[pl.ds(0, 16)] = cq[pl.ds(112, 16)]
    shift_s[pl.ds(16, 16)] = gc[pl.ds(112, 16)]
    ahead = remote(shift_s, shift_r, sems.at[0], sems.at[1], after)
    ahead.start()

    run_step(rings, 4)

    sub_w, lane_w = iota((128, 512), 0), iota((128, 512), 1)
    span_row = (sub_w == (((lane_w >> 2) + 127) & 127)).astype(F32).astype(BF16)
    lane_8 = iota((8, 512), 1)
    picked_row = jnp.where(
        (lane_8 & 2) == 0,
        dot(first_id[0:8], span_row, ((1,), (0,))),
        dot(second_id[0:8], span_row, ((1,), (0,))),
    )
    wanted_row = (picked_row * 2.0 + (lane_8 & 1).astype(F32))[0:1]
    sel_t[...] = jnp.where(iota((512, 512), 0).astype(F32) == wanted_row, 1.0, 0.0).astype(BF16)

    ahead.wait()
    row_1 = iota((128, 256), 0)
    shifted_in = shift_r[...].astype(F32)
    queries = jnp.where(
        row_1 == 0, shifted_in[15:16], pltpu.roll(cq[...].astype(F32), 1, 0)
    ).astype(BF16)
    place = row_1 + s * 128
    unmatched = (place >= 1) & (place < 64)
    grads = jnp.where(row_1 == 0, shifted_in[31:32], pltpu.roll(gc[...].astype(F32), 1, 0))
    grads = jnp.where(unmatched, 0.0, grads).astype(BF16)
    wait_all(sb, rb, 2)
    got = rb[...].astype(F32)
    near_keys = got[:, :8].reshape(512, 256).astype(BF16)
    near_values = got[:, 8:].reshape(512, 256).astype(BF16)
    mine = ((iota((512, 128), 0) & 4) != 0) == (iota((512, 128), 1) >= 64)
    outs, query_grads, key_grads, value_grads = [], [], [], []
    for head in range(2):
        cols = slice(head * 128, head * 128 + 128)
        k_h, v_h, q_h, g_h = near_keys[:, cols], near_values[:, cols], queries[:, cols], grads[:, cols]
        scores = jnp.where(mine, dot(k_h, q_h, ((1,), (1,))) * SCALE, LOW)
        numer = jnp.exp(scores - jnp.max(scores, axis=0, keepdims=True))
        probs = numer / jnp.sum(numer, axis=0, keepdims=True)
        weights = probs.astype(BF16)
        outs.append(dot(weights, v_h, ((0,), (0,))))
        grad_probs = dot(v_h, g_h, ((1,), (1,)))
        centre = jnp.sum(probs * grad_probs, axis=0, keepdims=True)
        grad_weights = (probs * (grad_probs - centre)).astype(BF16)
        query_grads.append(dot(grad_weights, k_h, ((0,), (0,))) * SCALE)
        key_grads.append(dot(grad_weights, q_h, ((1,), (0,))) * SCALE)
        value_grads.append(dot(weights, g_h, ((1,), (0,))))
    key_grads = jnp.concatenate(key_grads, axis=1).reshape(64, 8, 256)
    value_grads = jnp.concatenate(value_grads, axis=1).reshape(64, 8, 256)
    gs[...] = jnp.concatenate([key_grads, value_grads], axis=1).astype(BF16)
    gr[pl.ds(s, 1)] = gs[pl.ds(s, 1)]
    cross = jnp.where(unmatched, 0.0, jnp.concatenate(outs, axis=1))
    query_grads = jnp.concatenate(query_grads, axis=1)
    back_s[...] = query_grads[0:8]
    back = remote(back_s, back_r, sems.at[4], sems.at[5], before)
    back.start()
    start_all(gs, gr, 6)

    cross_rows = cross.astype(BF16)

    def project(dx, half):
        column = (lax.rem(x + dx, 4) * 2 + half) * 512
        return dot(cross_rows, w[:, pl.ds(pl.multiple_of(column, 512), 512)], ((1,), (0,)))

    def to_sibling(dx):
        return remote(pair_s.at[dx], pair_r.at[dx], pair_ss.at[dx], pair_rs.at[dx], sibling)

    for dx in (2, 1, 3, 0):
        pair_s[dx] = project(dx, 1 - core).astype(BF16)
        to_sibling(dx).start()
    for dx in (2, 1, 3, 0):
        own_part = project(dx, core)
        to_sibling(dx).wait_recv()
        part_s[dx] = (own_part + pair_r[dx].astype(F32)).astype(BF16)
        if dx:
            remote(part_s.at[dx], part_r.at[dx], sems.at[12], sems.at[13], same_core(s, dx)).start()
        edge = part_s.at[dx, pl.ds(0, 16)]
        remote(edge, edge_r.at[dx], sems.at[14], sems.at[15], same_core(before[0], dx)).start()

    for ring in rings:
        ring.finish()
    q_low = yr[:, q_rows].reshape(1024, 128)

    def keys_of(d, first):
        k_h, v_h = zr[pl.ds(d, 1), k_rows].reshape(128, 128), zr[pl.ds(d, 1), v_rows].reshape(128, 128)
        scores = dot(k_h, q_low, ((1,), (1,))) * SCALE
        if first:
            key, query = iota((128, 1024), 0), iota((128, 1024), 1)
            block = query >> 7
            allowed = ((block == 0) & (key <= query)) | (block > y)
            scores = jnp.where(allowed, scores, LOW)
            top_new = jnp.max(scores, axis=0, keepdims=True)
            numer = jnp.where(allowed, jnp.exp(scores - top_new), 0.0)
            total[...] = jnp.sum(numer, axis=0, keepdims=True)
            acc[...] = dot(v_h, numer.astype(BF16), ((0,), (0,)))
        else:
            top_old = top[...]
            top_new = jnp.maximum(top_old, jnp.max(scores, axis=0, keepdims=True))
            fade = jnp.exp(top_old - top_new)
            numer = jnp.exp(scores - top_new)
            total[...] = total[...] * fade + jnp.sum(numer, axis=0, keepdims=True)
            acc[...] = acc[...] * fade + dot(v_h, numer.astype(BF16), ((0,), (0,)))
        top[...] = top_new

    keys_of(0, True)

    def later_keys(d, _):
        keys_of(d, False)
        return 0

    lax.fori_loop(1, z + 1, later_keys, 0)
    pad = jnp.zeros((6, 128), F32)
    for e in range(8):
        cols = slice(e * 128, e * 128 + 128)
        oy_s[e] = acc[:, cols].astype(BF16)
        sy_s[e] = jnp.concatenate([top[:, cols], total[:, cols], pad], axis=0)
    for e in (4, 3, 5, 2, 6, 1, 7):
        owner = (shifted_seq(s, 0, 8 - e), h)
        remote(oy_s.at[e], oy_r.at[e], sems.at[8], sems.at[9], owner).start()
        remote(sy_s.at[e], sy_r.at[e], sems.at[10], sems.at[11], owner).start()

    k_high = yr[:, k_rows].reshape(1024, 128)
    v_high = yr[:, v_rows].reshape(1024, 128)

    def queries_of(d, first):
        scores = dot(k_high, zr[pl.ds(d, 1), q_rows].reshape(128, 128), ((1,), (1,))) * SCALE
        if first:
            key, query = iota((1024, 128), 0), iota((1024, 128), 1)
            block = key >> 7
            allowed = (key <= query) | ((block >= 1) & (block <= y))
            scores = jnp.where(allowed, scores, LOW)
        best = jnp.max(scores, axis=0, keepdims=True)
        numer = jnp.exp(scores - best)
        whole = jnp.sum(numer, axis=0, keepdims=True)
        out = dot(v_high, numer.astype(BF16), ((0,), (0,)))
        return best, whole, out

    def move_z(d):
        owner = (shifted_seq(s, 8 - d, 0), h)
        return (
            remote(oz_s.at[d], oz_r.at[d], oz_ss.at[d], oz_rs.at[d], owner),
            remote(sz_s.at[d], sz_r.at[d], sz_ss.at[d], sz_rs.at[d], owner),
        )

    def later_queries(d, _):
        best, whole, out = queries_of(d, False)
        oz_s[pl.ds(d, 1)] = out.astype(BF16)[None]
        sz_s[pl.ds(d, 1)] = jnp.concatenate([best, whole, pad], axis=0)[None]
        for copy in move_z(d):
            copy.start()
        return 0

    lax.fori_loop(z + 1, 8, later_queries, 0)
    own_high = queries_of(0, True)

    others = pl.ds(1, 7)
    neighbour = (shifted_seq(s, 0, 1), h)
    remote(oy_s.at[others], oy_r.at[others], sems.at[8], sems.at[9], neighbour).wait()
    remote(sy_s.at[others], sy_r.at[others], sems.at[10], sems.at[11], neighbour).wait()
    stats = [sy_s[0]] + [sy_r[e] for e in range(1, 8)]
    best = functools.reduce(jnp.maximum, [stat[0:1] for stat in stats])
    fades = [jnp.exp(stat[0:1] - best) for stat in stats]
    whole = sum(stat[1:2] * fade for stat, fade in zip(stats, fades))
    summed = oy_s[0].astype(F32) * fades[0]
    for e in range(1, 8):
        summed += oy_r[e].astype(F32) * fades[e]
    out_low = jnp.transpose(summed / whole)

    def merge_z(d, carry):
        best, whole, out = carry
        for copy in move_z(d):
            copy.wait_recv()
        stat = sz_r[pl.ds(d, 1)].reshape(8, 128)
        best_new = jnp.maximum(best, stat[0:1])
        fade, fade_in = jnp.exp(best - best_new), jnp.exp(stat[0:1] - best_new)
        out_in = oz_r[pl.ds(d, 1)].reshape(128, 128).astype(F32)
        return best_new, whole * fade + stat[1:2] * fade_in, out * fade + out_in * fade_in

    best, whole, out = lax.fori_loop(8 - z, 8, merge_z, own_high)
    out_high = jnp.transpose(out / whole)
    so_v[...] = jnp.concatenate([out_low, out_high], axis=1).astype(BF16)
    out_so = pltpu.make_async_copy(so_v, self_out, out_sem.at[1])
    out_so.start()

    three, four = pl.ds(1, 3), pl.ds(0, 4)
    remote(part_s.at[three], part_r.at[three], sems.at[12], sems.at[13], same_core(s, 1)).wait()
    remote(
        part_s.at[four, pl.ds(0, 16)], edge_r.at[four], sems.at[14], sems.at[15], same_core(before[0], 1)
    ).wait()
    for dx in range(4):
        to_sibling(dx).wait_send()
    summed, edge = part_s[0].astype(F32), edge_r[0].astype(F32)
    for dx in range(1, 4):
        summed += part_r[dx].astype(F32)
        edge += edge_r[dx].astype(F32)
    pr_v[...] = jnp.where(
        iota((128, 512), 0) == 127, edge[0:1], pltpu.roll(summed, 127, 0)
    ).astype(BF16)
    out_pr = pltpu.make_async_copy(pr_v, projected, out_sem.at[2])
    out_pr.start()

    back.wait()
    dq_v[...] = jnp.where(row_1 == 127, back_r[0:1], pltpu.roll(query_grads, 127, 0))
    out_dq = pltpu.make_async_copy(dq_v, grad_q, out_sem.at[0])
    out_dq.start()

    def sent_z(d, _):
        for copy in move_z(d):
            copy.wait_send()
        return 0

    lax.fori_loop(z + 1, 8, sent_z, 0)
    for ring in rings:
        ring.finish_sends()

    wait_all(gs, gr, 6)
    returned = gr[...].astype(F32)
    chosen = sel_t[...]
    copies = [out_dq, out_so, out_pr]
    for i, (held, out, piece) in enumerate(
        ((dk_v, grad_k, returned[:, :8]), (dv_v, grad_v, returned[:, 8:]))
    ):
        rows = piece.reshape(512, 256).astype(BF16)
        held[...] = dot(chosen, rows, ((1,), (0,))).astype(BF16).reshape(256, 2, 256)
        copies.append(pltpu.make_async_copy(held, out, out_sem.at[3 + i]))
        copies[-1].start()
    for copy in copies:
        copy.wait()


def hand_over(*refs):
    sources, targets, held, sem = refs[:5], refs[5:10], refs[10:15], refs[15]
    reads = [pltpu.make_async_copy(a, b, sem.at[0, i]) for i, (a, b) in enumerate(zip(sources, held))]
    writes = [pltpu.make_async_copy(a, b, sem.at[1, i]) for i, (a, b) in enumerate(zip(held, targets))]
    for read in reads:
        read.start()
    for read, write in zip(reads, writes):
        read.wait()
        write.start()
    for write in writes:
        write.wait()


def shards(sq, sk, sv, cq, store_k, store_v, ids, w, go):
    any_space = pl.BlockSpec(memory_space=pl.ANY)
    vmem = pl.BlockSpec(memory_space=pltpu.VMEM)
    V = pltpu.VMEM
    dma = pltpu.SemaphoreType.DMA
    shapes = (
        jax.ShapeDtypeStruct((128, 256), BF16),
        jax.ShapeDtypeStruct((128, 512), BF16),
        jax.ShapeDtypeStruct((128, 256), F32),
        jax.ShapeDtypeStruct((256, 2, 256), BF16),
        jax.ShapeDtypeStruct((256, 2, 256), BF16),
    )
    results = pl.pallas_call(
        body,
        name="retrieval_attention",
        out_shape=shapes,
        in_specs=[any_space] * 6 + [vmem] + [any_space] * 2,
        out_specs=(any_space,) * 5,
        scratch_shapes=[
            V((8, 384, 128), BF16),
            V((8, 384, 128), BF16),
            V((128, 256), BF16),
            V((256, 2, 256), BF16),
            V((256, 2, 256), BF16),
            V((256, 4096), BF16),
            V((128, 4096), BF16),
            V((512, 512), BF16),
            V((64, 16, 256), BF16),
            V((64, 16, 256), BF16),
            V((64, 16, 256), BF16),
            V((64, 16, 256), BF16),
            V((128, 256), BF16),
            V((32, 256), BF16),
            V((32, 256), BF16),
            V((8, 256), F32),
            V((8, 256), F32),
            V((128, 1024), F32),
            V((1, 1024), F32),
            V((1, 1024), F32),
            V((8, 128, 128), BF16),
            V((8, 128, 128), BF16),
            V((8, 8, 128), F32),
            V((8, 8, 128), F32),
            V((8, 128, 128), BF16),
            V((8, 128, 128), BF16),
            V((8, 8, 128), F32),
            V((8, 8, 128), F32),
            V((4, 128, 512), BF16),
            V((4, 128, 512), BF16),
            V((4, 128, 512), BF16),
            V((4, 128, 512), BF16),
            V((4, 16, 512), BF16),
            V((128, 256), BF16),
            V((128, 512), BF16),
            V((128, 256), F32),
            V((256, 2, 256), BF16),
            V((256, 2, 256), BF16),
            dma((11,)),
            dma((2, 5, CHUNKS)),
            dma((2, 5, CHUNKS)),
            dma((2, 5, CHUNKS)),
            dma((2, 5, CHUNKS)),
            dma((8,)),
            dma((8,)),
            dma((8,)),
            dma((8,)),
            dma((4,)),
            dma((4,)),
            dma((16,)),
            dma((5,)),
            pltpu.SemaphoreType.REGULAR,
        ],
        compiler_params=pltpu.CompilerParams(
            collective_id=0, has_side_effects=True, vmem_limit_bytes=60 << 20
        ),
    )(sq, sk, sv, cq, store_k, store_v, ids.T, w, go)
    return pl.pallas_call(
        hand_over,
        name="hand_over",
        out_shape=shapes,
        in_specs=[any_space] * 5,
        out_specs=(any_space,) * 5,
        scratch_shapes=[V(shape.shape, shape.dtype) for shape in shapes] + [dma((2, 5))],
        compiler_params=pltpu.CompilerParams(vmem_limit_bytes=60 << 20),
    )(*results)


def solution(mesh):
    by_token = P("seq", "heads")
    by_row = P(None, "seq", "heads")
    return jax.shard_map(
        shards,
        mesh=mesh,
        in_specs=(
            by_token, by_token, by_token, by_token, by_row, by_row, P(), P("heads", None), P("seq", None),
        ),
        out_specs=(by_token, by_token, by_token, by_row, by_row),
        check_vma=False,
    )
```

```python
import functools
import math

import jax
import jax.numpy as jnp
from jax import lax
from jax.experimental import pallas as pl
from jax.experimental.pallas import tpu as pltpu
from jax.sharding import PartitionSpec as P

MESH = pl.DeviceIdType.MESH
BF16 = jnp.bfloat16
F32 = jnp.float32
HEAD_DIM = 128
SCALE = 1.0 / math.sqrt(HEAD_DIM)
LOW = -1e30
CHUNKS = 2


def dot(a, b, dims):
    return lax.dot_general(a, b, (dims, ((), ())), preferred_element_type=F32)


def iota(shape, axis):
    return lax.broadcasted_iota(jnp.int32, shape, axis)


def remote(src, dst, send_sem, recv_sem, device):
    return pltpu.make_async_remote_copy(
        src_ref=src,
        dst_ref=dst,
        send_sem=send_sem,
        recv_sem=recv_sem,
        device_id=device,
        device_id_type=MESH,
    )


def shifted_seq(s, dz, dy):
    return lax.rem(s // 8 + dz, 8) * 8 + lax.rem(lax.rem(s, 8) + dy, 8)


def far_first(i):
    return lax.rem(4 + (1 - 2 * lax.rem(i, 2)) * ((i + 1) // 2), 8)


def only(needed, act):
    if needed is None:
        act()
    else:
        pl.when(needed)(act)


class Ring:
    def __init__(self, buf, send_sem, recv_sem, right, left, chunks, needs=None):
        self.buf, self.send_sem, self.recv_sem = buf, send_sem, recv_sem
        self.right, self.left, self.chunks = right, left, chunks
        self.needs = needs or (lambda *move: None)

    def copy(self, step, rightward, chunk):
        source, target = (step - 1, step) if rightward else ((9 - step) % 8, 8 - step)
        rows = pl.ds(*self.chunks[chunk])
        return remote(
            self.buf.at[source, rows],
            self.buf.at[target, rows],
            self.send_sem.at[int(rightward), step, chunk],
            self.recv_sem.at[int(rightward), step, chunk],
            self.right if rightward else self.left,
        )

    def moves(self, step):
        return [
            (rightward, chunk)
            for chunk in range(CHUNKS)
            for rightward in (True, False)
            if step < 4 or (chunk < CHUNKS // 2) == rightward
        ]

    def start(self, step, rightward, chunk):
        only(self.needs(step, rightward, chunk, True), self.copy(step, rightward, chunk).start)

    def received(self, step, rightward, chunk):
        only(self.needs(step, rightward, chunk, False), self.copy(step, rightward, chunk).wait_recv)

    def finish(self):
        for move in self.moves(4):
            self.received(4, *move)
        for move in self.moves(3):
            if move not in self.moves(4):
                self.received(3, *move)

    def finish_sends(self):
        for step in range(1, 5):
            for move in self.moves(step):
                only(self.needs(step, *move, True), self.copy(step, *move).wait_send)


def run_step(rings, step):
    for move in rings[0].moves(step):
        for ring in rings:
            if step > 1:
                ring.received(step - 1, *move)
            ring.start(step, *move)


def body(
    sq_in, sk_in, sv_in, cq_in, stk_in, stv_in, idt, w_in, go_in,
    self_out, projected, grad_q, grad_k, grad_v,
    zr, yr, cq, stk, stv, w, go,
    sel_t, sb, rb, gs, gr, gc, shift_s, shift_r, back_s, back_r,
    acc, top, total, oy_s, oy_r, sy_s, sy_r, oz_s, oz_r, sz_s, sz_r, part_s, part_r, pair_s, pair_r, edge_r,
    so_v, pr_v, dq_v, dk_v, dv_v,
    load_sem, z_ss, z_rs, y_ss, y_rs, oz_ss, oz_rs, sz_ss, sz_rs, pair_ss, pair_rs, sems, out_sem, plane_sem,
):
    s, h = lax.axis_index("seq"), lax.axis_index("heads")
    z, y = s // 8, lax.rem(s, 8)
    low, high = pl.ds(0, 128), pl.ds(128, 128)
    k_rows, v_rows, q_rows = pl.ds(0, 128), pl.ds(128, 128), pl.ds(256, 128)

    barrier = pltpu.get_barrier_semaphore()

    def greet_lines(k, _):
        step = far_first(k)
        for device in ((shifted_seq(s, step, 0), h), (shifted_seq(s, 0, step), h)):
            pl.semaphore_signal(barrier, inc=1, device_id=device, device_id_type=MESH)
        return 0

    lax.fori_loop(0, 7, greet_lines, 0)
    x, core = h // 2, lax.rem(h, 2)
    sibling = (s, h + 1 - 2 * core)

    def same_core(row, dx):
        return (row, lax.rem(x + dx, 4) * 2 + core)

    near = [sibling] + [same_core(s, dx) for dx in (1, 2, 3)]
    near += [same_core(row, dx) for row in (lax.rem(s + 1, 64), lax.rem(s + 63, 64)) for dx in range(4)]
    for device in near:
        pl.semaphore_signal(barrier, inc=1, device_id=device, device_id_type=MESH)

    def load(i, src, dst):
        return pltpu.make_async_copy(src, dst, load_sem.at[i])

    z_own = (sk_in.at[:, low], sv_in.at[:, low], sq_in.at[:, high])
    y_own = (sk_in.at[:, high], sv_in.at[:, high], sq_in.at[:, low])
    parts = (k_rows, v_rows, q_rows)
    loads = [load(0, stk_in, stk), load(1, stv_in, stv), load(2, go_in, go), load(3, w_in, w), load(4, cq_in, cq)]
    loads += [load(5 + i, z_own[i], zr.at[0, parts[i]]) for i in range(3)]
    loads += [load(8 + i, y_own[i], yr.at[0, parts[i]]) for i in range(3)]
    for copy in loads[5:] + loads[:5]:
        copy.start()


    pl.semaphore_wait(barrier, 26)

    def greet_plane(k, _):
        device = (shifted_seq(s, far_first(k), 0), h)
        pl.semaphore_signal(plane_sem, inc=1, device_id=device, device_id_type=MESH)
        return 0

    lax.fori_loop(0, 7, greet_plane, 0)

    def needs_z(step, rightward, chunk, sending):
        at = step - 1 if sending else step
        if rightward and chunk == 0:
            return (z >= at) & (z <= 6) if sending else z >= at
        if not rightward and chunk == 1:
            return (z + at <= 7) & (z >= 1) if sending else z + at <= 7
        if rightward:
            return lax.rem(z + 8 - at, 8) >= 5
        return lax.rem(z + at, 8) <= 2

    rings = (
        Ring(
            zr, z_ss, z_rs, (shifted_seq(s, 1, 0), h), (shifted_seq(s, 7, 0), h), ((0, 256), (256, 128)), needs_z
        ),
        Ring(yr, y_ss, y_rs, (shifted_seq(s, 0, 1), h), (shifted_seq(s, 0, 7), h), ((0, 192), (192, 192))),
    )
    for copy in loads[5:]:
        copy.wait()
    run_step(rings, 1)

    ids = idt[...].astype(F32)
    first_id = jnp.broadcast_to(ids[0:1], (128, 128)).astype(BF16)
    second_id = jnp.broadcast_to(ids[1:2], (128, 128)).astype(BF16)
    sub, lane = iota((512, 128), 0), iota((512, 128), 1)
    span_of = (lane == (((sub >> 2) + 127) & 127)).astype(F32).astype(BF16)
    picked = jnp.where(
        (sub & 2) == 0,
        dot(span_of, first_id, ((1,), (1,))),
        dot(span_of, second_id, ((1,), (1,))),
    )
    wanted = picked * 2.0 + (sub & 1).astype(F32)
    lane_f = lane.astype(F32)
    sel = jnp.concatenate(
        [jnp.where(wanted == lane_f + 128.0 * c, 1.0, 0.0).astype(BF16) for c in range(4)], axis=1
    )
    loads[0].wait()
    keys_out = dot(sel, stk[...].reshape(512, 256), ((1,), (0,)))
    loads[1].wait()
    values_out = dot(sel, stv[...].reshape(512, 256), ((1,), (0,)))
    sb[...] = jnp.concatenate(
        [keys_out.reshape(64, 8, 256), values_out.reshape(64, 8, 256)], axis=1
    ).astype(BF16)
    rb[pl.ds(s, 1)] = sb[pl.ds(s, 1)]


    def send(source, target, which, dz, dy):
        to = shifted_seq(s, dz, dy)
        remote(source.at[to], target.at[s], sems.at[which], sems.at[which + 1], (to, h)).start()

    def start_lines(source, target, which):
        def one(k, _):
            step = far_first(k)
            send(source, target, which, step, 0)
            send(source, target, which, 0, step)
            return 0

        lax.fori_loop(0, 7, one, 0)

    def start_rest(source, target, which):
        def one(k, _):
            send(source, target, which, far_first(k // 7), far_first(lax.rem(k, 7)))
            return 0

        lax.fori_loop(0, 49, one, 0)

    def wait_all(source, target, which):
        rows = pl.ds(0, 63)
        remote(
            source.at[rows],
            target.at[rows],
            sems.at[which],
            sems.at[which + 1],
            (shifted_seq(s, 0, 1), h),
        ).wait()

    after = (lax.rem(s + 1, 64), h)
    before = (lax.rem(s + 63, 64), h)

    start_lines(sb, rb, 2)
    pl.semaphore_wait(plane_sem, 7)
    start_rest(sb, rb, 2)

    run_step(rings, 2)


    run_step(rings, 3)

    loads[2].wait()
    loads[3].wait()
    gc[...] = dot(go[...], w[...], ((1,), (1,))).astype(BF16)
    loads[4].wait()
    shift_s[pl.ds(0, 16)] = cq[pl.ds(112, 16)]
    shift_s[pl.ds(16, 16)] = gc[pl.ds(112, 16)]
    ahead = remote(shift_s, shift_r, sems.at[0], sems.at[1], after)
    ahead.start()

    run_step(rings, 4)

    sub_w, lane_w = iota((128, 512), 0), iota((128, 512), 1)
    span_row = (sub_w == (((lane_w >> 2) + 127) & 127)).astype(F32).astype(BF16)
    lane_8 = iota((8, 512), 1)
    picked_row = jnp.where(
        (lane_8 & 2) == 0,
        dot(first_id[0:8], span_row, ((1,), (0,))),
        dot(second_id[0:8], span_row, ((1,), (0,))),
    )
    wanted_row = (picked_row * 2.0 + (lane_8 & 1).astype(F32))[0:1]
    sel_t[...] = jnp.where(iota((512, 512), 0).astype(F32) == wanted_row, 1.0, 0.0).astype(BF16)

    ahead.wait()
    row_1 = iota((128, 256), 0)
    shifted_in = shift_r[...].astype(F32)
    queries = jnp.where(
        row_1 == 0, shifted_in[15:16], pltpu.roll(cq[...].astype(F32), 1, 0)
    ).astype(BF16)
    place = row_1 + s * 128
    unmatched = (place >= 1) & (place < 64)
    grads = jnp.where(row_1 == 0, shifted_in[31:32], pltpu.roll(gc[...].astype(F32), 1, 0))
    grads = jnp.where(unmatched, 0.0, grads).astype(BF16)
    wait_all(sb, rb, 2)
    got = rb[...].astype(F32)
    near_keys = got[:, :8].reshape(512, 256).astype(BF16)
    near_values = got[:, 8:].reshape(512, 256).astype(BF16)
    mine = ((iota((512, 128), 0) & 4) != 0) == (iota((512, 128), 1) >= 64)
    outs, query_grads, key_grads, value_grads = [], [], [], []
    for head in range(2):
        cols = slice(head * 128, head * 128 + 128)
        k_h, v_h, q_h, g_h = near_keys[:, cols], near_values[:, cols], queries[:, cols], grads[:, cols]
        scores = jnp.where(mine, dot(k_h, q_h, ((1,), (1,))) * SCALE, LOW)
        numer = jnp.exp(scores - jnp.max(scores, axis=0, keepdims=True))
        probs = numer / jnp.sum(numer, axis=0, keepdims=True)
        weights = probs.astype(BF16)
        outs.append(dot(weights, v_h, ((0,), (0,))))
        grad_probs = dot(v_h, g_h, ((1,), (1,)))
        centre = jnp.sum(probs * grad_probs, axis=0, keepdims=True)
        grad_weights = (probs * (grad_probs - centre)).astype(BF16)
        query_grads.append(dot(grad_weights, k_h, ((0,), (0,))) * SCALE)
        key_grads.append(dot(grad_weights, q_h, ((1,), (0,))) * SCALE)
        value_grads.append(dot(weights, g_h, ((1,), (0,))))
    key_grads = jnp.concatenate(key_grads, axis=1).reshape(64, 8, 256)
    value_grads = jnp.concatenate(value_grads, axis=1).reshape(64, 8, 256)
    gs[...] = jnp.concatenate([key_grads, value_grads], axis=1).astype(BF16)
    gr[pl.ds(s, 1)] = gs[pl.ds(s, 1)]
    cross = jnp.where(unmatched, 0.0, jnp.concatenate(outs, axis=1))
    query_grads = jnp.concatenate(query_grads, axis=1)
    back_s[...] = query_grads[0:8]
    back = remote(back_s, back_r, sems.at[4], sems.at[5], before)
    back.start()
    start_rest(gs, gr, 6)
    start_lines(gs, gr, 6)

    cross_rows = cross.astype(BF16)

    def project(dx, half):
        column = (lax.rem(x + dx, 4) * 2 + half) * 512
        return dot(cross_rows, w[:, pl.ds(pl.multiple_of(column, 512), 512)], ((1,), (0,)))

    def to_sibling(dx):
        return remote(pair_s.at[dx], pair_r.at[dx], pair_ss.at[dx], pair_rs.at[dx], sibling)

    for dx in (2, 1, 3, 0):
        pair_s[dx] = project(dx, 1 - core).astype(BF16)
        to_sibling(dx).start()
    for dx in (2, 1, 3, 0):
        own_part = project(dx, core)
        to_sibling(dx).wait_recv()
        part_s[dx] = (own_part + pair_r[dx].astype(F32)).astype(BF16)
        if dx:
            remote(part_s.at[dx], part_r.at[dx], sems.at[12], sems.at[13], same_core(s, dx)).start()
        edge = part_s.at[dx, pl.ds(0, 16)]
        remote(edge, edge_r.at[dx], sems.at[14], sems.at[15], same_core(before[0], dx)).start()

    for ring in rings:
        ring.finish()
    q_low = yr[:, q_rows].reshape(1024, 128)

    def keys_of(d, first):
        k_h, v_h = zr[pl.ds(d, 1), k_rows].reshape(128, 128), zr[pl.ds(d, 1), v_rows].reshape(128, 128)
        scores = dot(k_h, q_low, ((1,), (1,))) * SCALE
        if first:
            key, query = iota((128, 1024), 0), iota((128, 1024), 1)
            block = query >> 7
            allowed = ((block == 0) & (key <= query)) | (block > y)
            scores = jnp.where(allowed, scores, LOW)
            top_new = jnp.max(scores, axis=0, keepdims=True)
            numer = jnp.where(allowed, jnp.exp(scores - top_new), 0.0)
            total[...] = jnp.sum(numer, axis=0, keepdims=True)
            acc[...] = dot(v_h, numer.astype(BF16), ((0,), (0,)))
        else:
            top_old = top[...]
            top_new = jnp.maximum(top_old, jnp.max(scores, axis=0, keepdims=True))
            fade = jnp.exp(top_old - top_new)
            numer = jnp.exp(scores - top_new)
            total[...] = total[...] * fade + jnp.sum(numer, axis=0, keepdims=True)
            acc[...] = acc[...] * fade + dot(v_h, numer.astype(BF16), ((0,), (0,)))
        top[...] = top_new

    keys_of(0, True)

    def later_keys(d, _):
        keys_of(d, False)
        return 0

    lax.fori_loop(1, z + 1, later_keys, 0)
    pad = jnp.zeros((6, 128), F32)
    for e in range(8):
        cols = slice(e * 128, e * 128 + 128)
        oy_s[e] = acc[:, cols].astype(BF16)
        sy_s[e] = jnp.concatenate([top[:, cols], total[:, cols], pad], axis=0)
    for e in (4, 3, 5, 2, 6, 1, 7):
        owner = (shifted_seq(s, 0, 8 - e), h)
        remote(oy_s.at[e], oy_r.at[e], sems.at[8], sems.at[9], owner).start()
        remote(sy_s.at[e], sy_r.at[e], sems.at[10], sems.at[11], owner).start()

    k_high = yr[:, k_rows].reshape(1024, 128)
    v_high = yr[:, v_rows].reshape(1024, 128)

    def queries_of(d, first):
        scores = dot(k_high, zr[pl.ds(d, 1), q_rows].reshape(128, 128), ((1,), (1,))) * SCALE
        if first:
            key, query = iota((1024, 128), 0), iota((1024, 128), 1)
            block = key >> 7
            allowed = (key <= query) | ((block >= 1) & (block <= y))
            scores = jnp.where(allowed, scores, LOW)
        best = jnp.max(scores, axis=0, keepdims=True)
        numer = jnp.exp(scores - best)
        whole = jnp.sum(numer, axis=0, keepdims=True)
        out = dot(v_high, numer.astype(BF16), ((0,), (0,)))
        return best, whole, out

    def move_z(d):
        owner = (shifted_seq(s, 8 - d, 0), h)
        return (
            remote(oz_s.at[d], oz_r.at[d], oz_ss.at[d], oz_rs.at[d], owner),
            remote(sz_s.at[d], sz_r.at[d], sz_ss.at[d], sz_rs.at[d], owner),
        )

    def later_queries(d, _):
        best, whole, out = queries_of(d, False)
        oz_s[pl.ds(d, 1)] = out.astype(BF16)[None]
        sz_s[pl.ds(d, 1)] = jnp.concatenate([best, whole, pad], axis=0)[None]
        for copy in move_z(d):
            copy.start()
        return 0

    lax.fori_loop(z + 1, 8, later_queries, 0)
    own_high = queries_of(0, True)

    others = pl.ds(1, 7)
    neighbour = (shifted_seq(s, 0, 1), h)
    remote(oy_s.at[others], oy_r.at[others], sems.at[8], sems.at[9], neighbour).wait()
    remote(sy_s.at[others], sy_r.at[others], sems.at[10], sems.at[11], neighbour).wait()
    stats = [sy_s[0]] + [sy_r[e] for e in range(1, 8)]
    best = functools.reduce(jnp.maximum, [stat[0:1] for stat in stats])
    fades = [jnp.exp(stat[0:1] - best) for stat in stats]
    whole = sum(stat[1:2] * fade for stat, fade in zip(stats, fades))
    summed = oy_s[0].astype(F32) * fades[0]
    for e in range(1, 8):
        summed += oy_r[e].astype(F32) * fades[e]
    out_low = jnp.transpose(summed / whole)

    def merge_z(d, carry):
        best, whole, out = carry
        for copy in move_z(d):
            copy.wait_recv()
        stat = sz_r[pl.ds(d, 1)].reshape(8, 128)
        best_new = jnp.maximum(best, stat[0:1])
        fade, fade_in = jnp.exp(best - best_new), jnp.exp(stat[0:1] - best_new)
        out_in = oz_r[pl.ds(d, 1)].reshape(128, 128).astype(F32)
        return best_new, whole * fade + stat[1:2] * fade_in, out * fade + out_in * fade_in

    best, whole, out = lax.fori_loop(8 - z, 8, merge_z, own_high)
    out_high = jnp.transpose(out / whole)
    so_v[...] = jnp.concatenate([out_low, out_high], axis=1).astype(BF16)
    out_so = pltpu.make_async_copy(so_v, self_out, out_sem.at[1])
    out_so.start()

    three, four = pl.ds(1, 3), pl.ds(0, 4)
    remote(part_s.at[three], part_r.at[three], sems.at[12], sems.at[13], same_core(s, 1)).wait()
    remote(
        part_s.at[four, pl.ds(0, 16)], edge_r.at[four], sems.at[14], sems.at[15], same_core(before[0], 1)
    ).wait()
    for dx in range(4):
        to_sibling(dx).wait_send()
    summed, edge = part_s[0].astype(F32), edge_r[0].astype(F32)
    for dx in range(1, 4):
        summed += part_r[dx].astype(F32)
        edge += edge_r[dx].astype(F32)
    pr_v[...] = jnp.where(
        iota((128, 512), 0) == 127, edge[0:1], pltpu.roll(summed, 127, 0)
    ).astype(BF16)
    out_pr = pltpu.make_async_copy(pr_v, projected, out_sem.at[2])
    out_pr.start()

    back.wait()
    dq_v[...] = jnp.where(row_1 == 127, back_r[0:1], pltpu.roll(query_grads, 127, 0))
    out_dq = pltpu.make_async_copy(dq_v, grad_q, out_sem.at[0])
    out_dq.start()

    def sent_z(d, _):
        for copy in move_z(d):
            copy.wait_send()
        return 0

    lax.fori_loop(z + 1, 8, sent_z, 0)
    for ring in rings:
        ring.finish_sends()

    wait_all(gs, gr, 6)
    returned = gr[...].astype(F32)
    chosen = sel_t[...]
    copies = [out_dq, out_so, out_pr]
    for i, (held, out, piece) in enumerate(
        ((dk_v, grad_k, returned[:, :8]), (dv_v, grad_v, returned[:, 8:]))
    ):
        rows = piece.reshape(512, 256).astype(BF16)
        held[...] = dot(chosen, rows, ((1,), (0,))).astype(BF16).reshape(256, 2, 256)
        copies.append(pltpu.make_async_copy(held, out, out_sem.at[3 + i]))
        copies[-1].start()
    for copy in copies:
        copy.wait()


def hand_over(*refs):
    sources, targets, held, sem = refs[:5], refs[5:10], refs[10:15], refs[15]
    reads = [pltpu.make_async_copy(a, b, sem.at[0, i]) for i, (a, b) in enumerate(zip(sources, held))]
    writes = [pltpu.make_async_copy(a, b, sem.at[1, i]) for i, (a, b) in enumerate(zip(held, targets))]
    for read in reads:
        read.start()
    for read, write in zip(reads, writes):
        read.wait()
        write.start()
    for write in writes:
        write.wait()


def shards(sq, sk, sv, cq, store_k, store_v, ids, w, go):
    any_space = pl.BlockSpec(memory_space=pl.ANY)
    vmem = pl.BlockSpec(memory_space=pltpu.VMEM)
    V = pltpu.VMEM
    dma = pltpu.SemaphoreType.DMA
    shapes = (
        jax.ShapeDtypeStruct((128, 256), BF16),
        jax.ShapeDtypeStruct((128, 512), BF16),
        jax.ShapeDtypeStruct((128, 256), F32),
        jax.ShapeDtypeStruct((256, 2, 256), BF16),
        jax.ShapeDtypeStruct((256, 2, 256), BF16),
    )
    results = pl.pallas_call(
        body,
        name="retrieval_attention",
        out_shape=shapes,
        in_specs=[any_space] * 6 + [vmem] + [any_space] * 2,
        out_specs=(any_space,) * 5,
        scratch_shapes=[
            V((8, 384, 128), BF16),
            V((8, 384, 128), BF16),
            V((128, 256), BF16),
            V((256, 2, 256), BF16),
            V((256, 2, 256), BF16),
            V((256, 4096), BF16),
            V((128, 4096), BF16),
            V((512, 512), BF16),
            V((64, 16, 256), BF16),
            V((64, 16, 256), BF16),
            V((64, 16, 256), BF16),
            V((64, 16, 256), BF16),
            V((128, 256), BF16),
            V((32, 256), BF16),
            V((32, 256), BF16),
            V((8, 256), F32),
            V((8, 256), F32),
            V((128, 1024), F32),
            V((1, 1024), F32),
            V((1, 1024), F32),
            V((8, 128, 128), BF16),
            V((8, 128, 128), BF16),
            V((8, 8, 128), F32),
            V((8, 8, 128), F32),
            V((8, 128, 128), BF16),
            V((8, 128, 128), BF16),
            V((8, 8, 128), F32),
            V((8, 8, 128), F32),
            V((4, 128, 512), BF16),
            V((4, 128, 512), BF16),
            V((4, 128, 512), BF16),
            V((4, 128, 512), BF16),
            V((4, 16, 512), BF16),
            V((128, 256), BF16),
            V((128, 512), BF16),
            V((128, 256), F32),
            V((256, 2, 256), BF16),
            V((256, 2, 256), BF16),
            dma((11,)),
            dma((2, 5, CHUNKS)),
            dma((2, 5, CHUNKS)),
            dma((2, 5, CHUNKS)),
            dma((2, 5, CHUNKS)),
            dma((8,)),
            dma((8,)),
            dma((8,)),
            dma((8,)),
            dma((4,)),
            dma((4,)),
            dma((16,)),
            dma((5,)),
            pltpu.SemaphoreType.REGULAR,
        ],
        compiler_params=pltpu.CompilerParams(
            collective_id=0, has_side_effects=True, vmem_limit_bytes=60 << 20
        ),
    )(sq, sk, sv, cq, store_k, store_v, ids.T, w, go)
    return pl.pallas_call(
        hand_over,
        name="hand_over",
        out_shape=shapes,
        in_specs=[any_space] * 5,
        out_specs=(any_space,) * 5,
        scratch_shapes=[V(shape.shape, shape.dtype) for shape in shapes] + [dma((2, 5))],
        compiler_params=pltpu.CompilerParams(vmem_limit_bytes=60 << 20),
    )(*results)


def solution(mesh):
    by_token = P("seq", "heads")
    by_row = P(None, "seq", "heads")
    return jax.shard_map(
        shards,
        mesh=mesh,
        in_specs=(
            by_token, by_token, by_token, by_token, by_row, by_row, P(), P("heads", None), P("seq", None),
        ),
        out_specs=(by_token, by_token, by_token, by_row, by_row),
        check_vma=False,
    )
```

```python
import functools
import math

import jax
import jax.numpy as jnp
from jax import lax
from jax.experimental import pallas as pl
from jax.experimental.pallas import tpu as pltpu
from jax.sharding import PartitionSpec as P

MESH = pl.DeviceIdType.MESH
BF16 = jnp.bfloat16
F32 = jnp.float32
HEAD_DIM = 128
SCALE = 1.0 / math.sqrt(HEAD_DIM)
LOW = -1e30
CHUNKS = 2


def dot(a, b, dims):
    return lax.dot_general(a, b, (dims, ((), ())), preferred_element_type=F32)


def iota(shape, axis):
    return lax.broadcasted_iota(jnp.int32, shape, axis)


def remote(src, dst, send_sem, recv_sem, device):
    return pltpu.make_async_remote_copy(
        src_ref=src,
        dst_ref=dst,
        send_sem=send_sem,
        recv_sem=recv_sem,
        device_id=device,
        device_id_type=MESH,
    )


def shifted_seq(s, dz, dy):
    return lax.rem(s // 8 + dz, 8) * 8 + lax.rem(lax.rem(s, 8) + dy, 8)


def far_first(i):
    return lax.rem(4 + (1 - 2 * lax.rem(i, 2)) * ((i + 1) // 2), 8)


def only(needed, act):
    if needed is None:
        act()
    else:
        pl.when(needed)(act)


class Ring:
    def __init__(self, buf, send_sem, recv_sem, right, left, chunks, needs=None):
        self.buf, self.send_sem, self.recv_sem = buf, send_sem, recv_sem
        self.right, self.left, self.chunks = right, left, chunks
        self.needs = needs or (lambda *move: None)

    def copy(self, step, rightward, chunk):
        source, target = (step - 1, step) if rightward else ((9 - step) % 8, 8 - step)
        rows = pl.ds(*self.chunks[chunk])
        return remote(
            self.buf.at[source, rows],
            self.buf.at[target, rows],
            self.send_sem.at[int(rightward), step, chunk],
            self.recv_sem.at[int(rightward), step, chunk],
            self.right if rightward else self.left,
        )

    def moves(self, step):
        return [
            (rightward, chunk)
            for chunk in range(CHUNKS)
            for rightward in (True, False)
            if step < 4 or (chunk < CHUNKS // 2) == rightward
        ]

    def start(self, step, rightward, chunk):
        only(self.needs(step, rightward, chunk, True), self.copy(step, rightward, chunk).start)

    def received(self, step, rightward, chunk):
        only(self.needs(step, rightward, chunk, False), self.copy(step, rightward, chunk).wait_recv)

    def finish(self):
        for move in self.moves(4):
            self.received(4, *move)
        for move in self.moves(3):
            if move not in self.moves(4):
                self.received(3, *move)

    def finish_sends(self):
        for step in range(1, 5):
            for move in self.moves(step):
                only(self.needs(step, *move, True), self.copy(step, *move).wait_send)


def run_step(rings, step):
    for move in rings[0].moves(step):
        for ring in rings:
            if step > 1:
                ring.received(step - 1, *move)
            ring.start(step, *move)


def body(
    sq_in, sk_in, sv_in, cq_in, stk_in, stv_in, idt, w_in, go_in,
    self_out, projected, grad_q, grad_k, grad_v,
    zr, yr, cq, stk, stv, w, go,
    sel_t, sb, rb, gs, gr, gc, shift_s, shift_r, back_s, back_r,
    acc, top, total, oy_s, oy_r, sy_s, sy_r, oz_s, oz_r, sz_s, sz_r, part_s, part_r, pair_s, pair_r, edge_r,
    so_v, pr_v, dq_v, dk_v, dv_v,
    load_sem, z_ss, z_rs, y_ss, y_rs, oz_ss, oz_rs, sz_ss, sz_rs, pair_ss, pair_rs, sems, out_sem, plane_sem,
):
    s, h = lax.axis_index("seq"), lax.axis_index("heads")
    z, y = s // 8, lax.rem(s, 8)
    low, high = pl.ds(0, 128), pl.ds(128, 128)
    k_rows, v_rows, q_rows = pl.ds(0, 128), pl.ds(128, 128), pl.ds(256, 128)

    barrier = pltpu.get_barrier_semaphore()

    def greet_lines(k, _):
        step = far_first(k)
        for device in ((shifted_seq(s, step, 0), h), (shifted_seq(s, 0, step), h)):
            pl.semaphore_signal(barrier, inc=1, device_id=device, device_id_type=MESH)
        return 0

    lax.fori_loop(0, 7, greet_lines, 0)
    x, core = h // 2, lax.rem(h, 2)
    sibling = (s, h + 1 - 2 * core)

    def same_core(row, dx):
        return (row, lax.rem(x + dx, 4) * 2 + core)

    near = [sibling] + [same_core(s, dx) for dx in (1, 2, 3)]
    near += [same_core(row, dx) for row in (lax.rem(s + 1, 64), lax.rem(s + 63, 64)) for dx in range(4)]
    for device in near:
        pl.semaphore_signal(barrier, inc=1, device_id=device, device_id_type=MESH)

    def load(i, src, dst):
        return pltpu.make_async_copy(src, dst, load_sem.at[i])

    z_own = (sk_in.at[:, low], sv_in.at[:, low], sq_in.at[:, high])
    y_own = (sk_in.at[:, high], sv_in.at[:, high], sq_in.at[:, low])
    parts = (k_rows, v_rows, q_rows)
    loads = [load(0, stk_in, stk), load(1, stv_in, stv), load(2, go_in, go), load(3, w_in, w), load(4, cq_in, cq)]
    loads += [load(5 + i, z_own[i], zr.at[0, parts[i]]) for i in range(3)]
    loads += [load(8 + i, y_own[i], yr.at[0, parts[i]]) for i in range(3)]
    for copy in loads[5:] + loads[:5]:
        copy.start()


    pl.semaphore_wait(barrier, 26)

    def greet_plane(k, _):
        device = (shifted_seq(s, far_first(k), 0), h)
        pl.semaphore_signal(plane_sem, inc=1, device_id=device, device_id_type=MESH)
        return 0

    lax.fori_loop(0, 7, greet_plane, 0)

    def needs_z(step, rightward, chunk, sending):
        at = step - 1 if sending else step
        if rightward and chunk == 0:
            return (z >= at) & (z <= 6) if sending else z >= at
        if not rightward and chunk == 1:
            return (z + at <= 7) & (z >= 1) if sending else z + at <= 7
        if rightward:
            return lax.rem(z + 8 - at, 8) >= 5
        return lax.rem(z + at, 8) <= 2

    rings = (
        Ring(
            zr, z_ss, z_rs, (shifted_seq(s, 1, 0), h), (shifted_seq(s, 7, 0), h), ((0, 256), (256, 128)), needs_z
        ),
        Ring(yr, y_ss, y_rs, (shifted_seq(s, 0, 1), h), (shifted_seq(s, 0, 7), h), ((0, 192), (192, 192))),
    )
    for copy in loads[5:]:
        copy.wait()
    run_step(rings, 1)

    ids = idt[...].astype(F32)
    first_id = jnp.broadcast_to(ids[0:1], (128, 128)).astype(BF16)
    second_id = jnp.broadcast_to(ids[1:2], (128, 128)).astype(BF16)
    sub, lane = iota((512, 128), 0), iota((512, 128), 1)
    span_of = (lane == (((sub >> 2) + 127) & 127)).astype(F32).astype(BF16)
    picked = jnp.where(
        (sub & 2) == 0,
        dot(span_of, first_id, ((1,), (1,))),
        dot(span_of, second_id, ((1,), (1,))),
    )
    wanted = picked * 2.0 + (sub & 1).astype(F32)
    lane_f = lane.astype(F32)
    sel = jnp.concatenate(
        [jnp.where(wanted == lane_f + 128.0 * c, 1.0, 0.0).astype(BF16) for c in range(4)], axis=1
    )
    loads[0].wait()
    keys_out = dot(sel, stk[...].reshape(512, 256), ((1,), (0,)))
    loads[1].wait()
    values_out = dot(sel, stv[...].reshape(512, 256), ((1,), (0,)))
    sb[...] = jnp.concatenate(
        [keys_out.reshape(64, 8, 256), values_out.reshape(64, 8, 256)], axis=1
    ).astype(BF16)
    rb[pl.ds(s, 1)] = sb[pl.ds(s, 1)]


    def send(source, target, which, dz, dy):
        to = shifted_seq(s, dz, dy)
        remote(source.at[to], target.at[s], sems.at[which], sems.at[which + 1], (to, h)).start()

    def start_lines(source, target, which):
        def one(k, _):
            step = far_first(k)
            send(source, target, which, step, 0)
            send(source, target, which, 0, step)
            return 0

        lax.fori_loop(0, 7, one, 0)

    def start_rest(source, target, which):
        def one(k, _):
            send(source, target, which, far_first(k // 7), far_first(lax.rem(k, 7)))
            return 0

        lax.fori_loop(0, 49, one, 0)

    def wait_all(source, target, which):
        rows = pl.ds(0, 63)
        remote(
            source.at[rows],
            target.at[rows],
            sems.at[which],
            sems.at[which + 1],
            (shifted_seq(s, 0, 1), h),
        ).wait()

    after = (lax.rem(s + 1, 64), h)
    before = (lax.rem(s + 63, 64), h)

    start_lines(sb, rb, 2)
    pl.semaphore_wait(plane_sem, 7)
    start_rest(sb, rb, 2)

    run_step(rings, 2)


    run_step(rings, 3)

    loads[2].wait()
    loads[3].wait()
    gc[...] = dot(go[...], w[...], ((1,), (1,))).astype(BF16)
    loads[4].wait()
    shift_s[pl.ds(0, 16)] = cq[pl.ds(112, 16)]
    shift_s[pl.ds(16, 16)] = gc[pl.ds(112, 16)]
    ahead = remote(shift_s, shift_r, sems.at[0], sems.at[1], after)
    ahead.start()

    run_step(rings, 4)

    sub_w, lane_w = iota((128, 512), 0), iota((128, 512), 1)
    span_row = (sub_w == (((lane_w >> 2) + 127) & 127)).astype(F32).astype(BF16)
    lane_8 = iota((8, 512), 1)
    picked_row = jnp.where(
        (lane_8 & 2) == 0,
        dot(first_id[0:8], span_row, ((1,), (0,))),
        dot(second_id[0:8], span_row, ((1,), (0,))),
    )
    wanted_row = (picked_row * 2.0 + (lane_8 & 1).astype(F32))[0:1]
    sel_t[...] = jnp.where(iota((512, 512), 0).astype(F32) == wanted_row, 1.0, 0.0).astype(BF16)

    ahead.wait()
    row_1 = iota((128, 256), 0)
    shifted_in = shift_r[...].astype(F32)
    queries = jnp.where(
        row_1 == 0, shifted_in[15:16], pltpu.roll(cq[...].astype(F32), 1, 0)
    ).astype(BF16)
    place = row_1 + s * 128
    unmatched = (place >= 1) & (place < 64)
    grads = jnp.where(row_1 == 0, shifted_in[31:32], pltpu.roll(gc[...].astype(F32), 1, 0))
    grads = jnp.where(unmatched, 0.0, grads).astype(BF16)
    wait_all(sb, rb, 2)
    got = rb[...].astype(F32)
    near_keys = got[:, :8].reshape(512, 256).astype(BF16)
    near_values = got[:, 8:].reshape(512, 256).astype(BF16)
    mine = ((iota((512, 128), 0) & 4) != 0) == (iota((512, 128), 1) >= 64)
    outs, query_grads, key_grads, value_grads = [], [], [], []
    for head in range(2):
        cols = slice(head * 128, head * 128 + 128)
        k_h, v_h, q_h, g_h = near_keys[:, cols], near_values[:, cols], queries[:, cols], grads[:, cols]
        scores = jnp.where(mine, dot(k_h, q_h, ((1,), (1,))) * SCALE, LOW)
        numer = jnp.exp(scores - jnp.max(scores, axis=0, keepdims=True))
        probs = numer / jnp.sum(numer, axis=0, keepdims=True)
        weights = probs.astype(BF16)
        outs.append(dot(weights, v_h, ((0,), (0,))))
        grad_probs = dot(v_h, g_h, ((1,), (1,)))
        centre = jnp.sum(probs * grad_probs, axis=0, keepdims=True)
        grad_weights = (probs * (grad_probs - centre)).astype(BF16)
        query_grads.append(dot(grad_weights, k_h, ((0,), (0,))) * SCALE)
        key_grads.append(dot(grad_weights, q_h, ((1,), (0,))) * SCALE)
        value_grads.append(dot(weights, g_h, ((1,), (0,))))
    key_grads = jnp.concatenate(key_grads, axis=1).reshape(64, 8, 256)
    value_grads = jnp.concatenate(value_grads, axis=1).reshape(64, 8, 256)
    gs[...] = jnp.concatenate([key_grads, value_grads], axis=1).astype(BF16)
    gr[pl.ds(s, 1)] = gs[pl.ds(s, 1)]
    cross = jnp.where(unmatched, 0.0, jnp.concatenate(outs, axis=1))
    query_grads = jnp.concatenate(query_grads, axis=1)
    back_s[...] = query_grads[0:8]
    back = remote(back_s, back_r, sems.at[4], sems.at[5], before)
    back.start()
    start_rest(gs, gr, 6)
    start_lines(gs, gr, 6)

    cross_rows = cross.astype(BF16)

    def project(dx, half):
        column = (lax.rem(x + dx, 4) * 2 + half) * 512
        return dot(cross_rows, w[:, pl.ds(pl.multiple_of(column, 512), 512)], ((1,), (0,)))

    def to_sibling(dx):
        return remote(pair_s.at[dx], pair_r.at[dx], pair_ss.at[dx], pair_rs.at[dx], sibling)

    for dx in (2, 1, 3, 0):
        pair_s[dx] = project(dx, 1 - core).astype(BF16)
        to_sibling(dx).start()
    for dx in (2, 1, 3, 0):
        own_part = project(dx, core)
        to_sibling(dx).wait_recv()
        part_s[dx] = (own_part + pair_r[dx].astype(F32)).astype(BF16)
        if dx:
            remote(part_s.at[dx], part_r.at[dx], sems.at[12], sems.at[13], same_core(s, dx)).start()
        edge = part_s.at[dx, pl.ds(0, 16)]
        remote(edge, edge_r.at[dx], sems.at[14], sems.at[15], same_core(before[0], dx)).start()

    for ring in rings:
        ring.finish()
    q_low = yr[:, q_rows].reshape(1024, 128)

    def keys_of(d, first):
        k_h, v_h = zr[pl.ds(d, 1), k_rows].reshape(128, 128), zr[pl.ds(d, 1), v_rows].reshape(128, 128)
        scores = dot(k_h, q_low, ((1,), (1,))) * SCALE
        if first:
            key, query = iota((128, 1024), 0), iota((128, 1024), 1)
            block = query >> 7
            allowed = ((block == 0) & (key <= query)) | (block > y)
            scores = jnp.where(allowed, scores, LOW)
            top_new = jnp.max(scores, axis=0, keepdims=True)
            numer = jnp.where(allowed, jnp.exp(scores - top_new), 0.0)
            total[...] = jnp.sum(numer, axis=0, keepdims=True)
            acc[...] = dot(v_h, numer.astype(BF16), ((0,), (0,)))
        else:
            top_old = top[...]
            top_new = jnp.maximum(top_old, jnp.max(scores, axis=0, keepdims=True))
            fade = jnp.exp(top_old - top_new)
            numer = jnp.exp(scores - top_new)
            total[...] = total[...] * fade + jnp.sum(numer, axis=0, keepdims=True)
            acc[...] = acc[...] * fade + dot(v_h, numer.astype(BF16), ((0,), (0,)))
        top[...] = top_new

    keys_of(0, True)

    def later_keys(d, _):
        keys_of(d, False)
        return 0

    lax.fori_loop(1, z + 1, later_keys, 0)
    pad = jnp.zeros((6, 128), F32)
    for e in range(8):
        cols = slice(e * 128, e * 128 + 128)
        oy_s[e] = acc[:, cols].astype(BF16)
        sy_s[e] = jnp.concatenate([top[:, cols], total[:, cols], pad], axis=0)
    for e in (4, 3, 5, 2, 6, 1, 7):
        owner = (shifted_seq(s, 0, 8 - e), h)
        remote(oy_s.at[e], oy_r.at[e], sems.at[8], sems.at[9], owner).start()
        remote(sy_s.at[e], sy_r.at[e], sems.at[10], sems.at[11], owner).start()

    k_high = yr[:, k_rows].reshape(1024, 128)
    v_high = yr[:, v_rows].reshape(1024, 128)

    def queries_of(d, first):
        scores = dot(k_high, zr[pl.ds(d, 1), q_rows].reshape(128, 128), ((1,), (1,))) * SCALE
        if first:
            key, query = iota((1024, 128), 0), iota((1024, 128), 1)
            block = key >> 7
            allowed = (key <= query) | ((block >= 1) & (block <= y))
            scores = jnp.where(allowed, scores, LOW)
        best = jnp.max(scores, axis=0, keepdims=True)
        numer = jnp.exp(scores - best)
        whole = jnp.sum(numer, axis=0, keepdims=True)
        out = dot(v_high, numer.astype(BF16), ((0,), (0,)))
        return best, whole, out

    def move_z(d):
        owner = (shifted_seq(s, 8 - d, 0), h)
        return (
            remote(oz_s.at[d], oz_r.at[d], oz_ss.at[d], oz_rs.at[d], owner),
            remote(sz_s.at[d], sz_r.at[d], sz_ss.at[d], sz_rs.at[d], owner),
        )

    def later_queries(d, _):
        best, whole, out = queries_of(d, False)
        oz_s[pl.ds(d, 1)] = out.astype(BF16)[None]
        sz_s[pl.ds(d, 1)] = jnp.concatenate([best, whole, pad], axis=0)[None]
        for copy in move_z(d):
            copy.start()
        return 0

    lax.fori_loop(z + 1, 8, later_queries, 0)
    own_high = queries_of(0, True)

    three, four = pl.ds(1, 3), pl.ds(0, 4)
    remote(part_s.at[three], part_r.at[three], sems.at[12], sems.at[13], same_core(s, 1)).wait()
    remote(
        part_s.at[four, pl.ds(0, 16)], edge_r.at[four], sems.at[14], sems.at[15], same_core(before[0], 1)
    ).wait()
    for dx in range(4):
        to_sibling(dx).wait_send()
    summed, edge = part_s[0].astype(F32), edge_r[0].astype(F32)
    for dx in range(1, 4):
        summed += part_r[dx].astype(F32)
        edge += edge_r[dx].astype(F32)
    pr_v[...] = jnp.where(
        iota((128, 512), 0) == 127, edge[0:1], pltpu.roll(summed, 127, 0)
    ).astype(BF16)
    out_pr = pltpu.make_async_copy(pr_v, projected, out_sem.at[2])
    out_pr.start()

    back.wait()
    dq_v[...] = jnp.where(row_1 == 127, back_r[0:1], pltpu.roll(query_grads, 127, 0))
    out_dq = pltpu.make_async_copy(dq_v, grad_q, out_sem.at[0])
    out_dq.start()

    wait_all(gs, gr, 6)
    returned = gr[...].astype(F32)
    chosen = sel_t[...]
    copies = [out_dq, out_pr]
    for i, (held, out, piece) in enumerate(
        ((dk_v, grad_k, returned[:, :8]), (dv_v, grad_v, returned[:, 8:]))
    ):
        rows = piece.reshape(512, 256).astype(BF16)
        held[...] = dot(chosen, rows, ((1,), (0,))).astype(BF16).reshape(256, 2, 256)
        copies.append(pltpu.make_async_copy(held, out, out_sem.at[3 + i]))
        copies[-1].start()

    others = pl.ds(1, 7)
    neighbour = (shifted_seq(s, 0, 1), h)
    remote(oy_s.at[others], oy_r.at[others], sems.at[8], sems.at[9], neighbour).wait()
    remote(sy_s.at[others], sy_r.at[others], sems.at[10], sems.at[11], neighbour).wait()
    stats = [sy_s[0]] + [sy_r[e] for e in range(1, 8)]
    best = functools.reduce(jnp.maximum, [stat[0:1] for stat in stats])
    fades = [jnp.exp(stat[0:1] - best) for stat in stats]
    whole = sum(stat[1:2] * fade for stat, fade in zip(stats, fades))
    summed = oy_s[0].astype(F32) * fades[0]
    for e in range(1, 8):
        summed += oy_r[e].astype(F32) * fades[e]
    out_low = jnp.transpose(summed / whole)

    def merge_z(d, carry):
        best, whole, out = carry
        for copy in move_z(d):
            copy.wait_recv()
        stat = sz_r[pl.ds(d, 1)].reshape(8, 128)
        best_new = jnp.maximum(best, stat[0:1])
        fade, fade_in = jnp.exp(best - best_new), jnp.exp(stat[0:1] - best_new)
        out_in = oz_r[pl.ds(d, 1)].reshape(128, 128).astype(F32)
        return best_new, whole * fade + stat[1:2] * fade_in, out * fade + out_in * fade_in

    best, whole, out = lax.fori_loop(8 - z, 8, merge_z, own_high)
    out_high = jnp.transpose(out / whole)
    so_v[...] = jnp.concatenate([out_low, out_high], axis=1).astype(BF16)
    out_so = pltpu.make_async_copy(so_v, self_out, out_sem.at[1])
    out_so.start()

    def sent_z(d, _):
        for copy in move_z(d):
            copy.wait_send()
        return 0

    lax.fori_loop(z + 1, 8, sent_z, 0)
    for ring in rings:
        ring.finish_sends()

    for copy in copies + [out_so]:
        copy.wait()


def hand_over(*refs):
    sources, targets, held, sem = refs[:5], refs[5:10], refs[10:15], refs[15]
    reads = [pltpu.make_async_copy(a, b, sem.at[0, i]) for i, (a, b) in enumerate(zip(sources, held))]
    writes = [pltpu.make_async_copy(a, b, sem.at[1, i]) for i, (a, b) in enumerate(zip(held, targets))]
    for read in reads:
        read.start()
    for read, write in zip(reads, writes):
        read.wait()
        write.start()
    for write in writes:
        write.wait()


def shards(sq, sk, sv, cq, store_k, store_v, ids, w, go):
    any_space = pl.BlockSpec(memory_space=pl.ANY)
    vmem = pl.BlockSpec(memory_space=pltpu.VMEM)
    V = pltpu.VMEM
    dma = pltpu.SemaphoreType.DMA
    shapes = (
        jax.ShapeDtypeStruct((128, 256), BF16),
        jax.ShapeDtypeStruct((128, 512), BF16),
        jax.ShapeDtypeStruct((128, 256), F32),
        jax.ShapeDtypeStruct((256, 2, 256), BF16),
        jax.ShapeDtypeStruct((256, 2, 256), BF16),
    )
    results = pl.pallas_call(
        body,
        name="retrieval_attention",
        out_shape=shapes,
        in_specs=[any_space] * 6 + [vmem] + [any_space] * 2,
        out_specs=(any_space,) * 5,
        scratch_shapes=[
            V((8, 384, 128), BF16),
            V((8, 384, 128), BF16),
            V((128, 256), BF16),
            V((256, 2, 256), BF16),
            V((256, 2, 256), BF16),
            V((256, 4096), BF16),
            V((128, 4096), BF16),
            V((512, 512), BF16),
            V((64, 16, 256), BF16),
            V((64, 16, 256), BF16),
            V((64, 16, 256), BF16),
            V((64, 16, 256), BF16),
            V((128, 256), BF16),
            V((32, 256), BF16),
            V((32, 256), BF16),
            V((8, 256), F32),
            V((8, 256), F32),
            V((128, 1024), F32),
            V((1, 1024), F32),
            V((1, 1024), F32),
            V((8, 128, 128), BF16),
            V((8, 128, 128), BF16),
            V((8, 8, 128), F32),
            V((8, 8, 128), F32),
            V((8, 128, 128), BF16),
            V((8, 128, 128), BF16),
            V((8, 8, 128), F32),
            V((8, 8, 128), F32),
            V((4, 128, 512), BF16),
            V((4, 128, 512), BF16),
            V((4, 128, 512), BF16),
            V((4, 128, 512), BF16),
            V((4, 16, 512), BF16),
            V((128, 256), BF16),
            V((128, 512), BF16),
            V((128, 256), F32),
            V((256, 2, 256), BF16),
            V((256, 2, 256), BF16),
            dma((11,)),
            dma((2, 5, CHUNKS)),
            dma((2, 5, CHUNKS)),
            dma((2, 5, CHUNKS)),
            dma((2, 5, CHUNKS)),
            dma((8,)),
            dma((8,)),
            dma((8,)),
            dma((8,)),
            dma((4,)),
            dma((4,)),
            dma((16,)),
            dma((5,)),
            pltpu.SemaphoreType.REGULAR,
        ],
        compiler_params=pltpu.CompilerParams(
            collective_id=0, has_side_effects=True, vmem_limit_bytes=60 << 20
        ),
    )(sq, sk, sv, cq, store_k, store_v, ids.T, w, go)
    return pl.pallas_call(
        hand_over,
        name="hand_over",
        out_shape=shapes,
        in_specs=[any_space] * 5,
        out_specs=(any_space,) * 5,
        scratch_shapes=[V(shape.shape, shape.dtype) for shape in shapes] + [dma((2, 5))],
        compiler_params=pltpu.CompilerParams(vmem_limit_bytes=60 << 20),
    )(*results)


def solution(mesh):
    by_token = P("seq", "heads")
    by_row = P(None, "seq", "heads")
    return jax.shard_map(
        shards,
        mesh=mesh,
        in_specs=(
            by_token, by_token, by_token, by_token, by_row, by_row, P(), P("heads", None), P("seq", None),
        ),
        out_specs=(by_token, by_token, by_token, by_row, by_row),
        check_vma=False,
    )
```
